512 devices in a mesh: mn: 32 (over y, z_hi, x), az: 16 (over z_lo, core).
Axes of the slice: x: 4, y: 4, z: 16 (z_hi: 2, z_lo: 8; z = z_hi * 8 + z_lo), core: 2. Of those that a mesh axis runs over, the one named last changes fastest.
Arguments:
- flow_state: float32 [41, 256, 128, 128], P(None, 'mn', 'az'), may hold values from -12 to 12, as said below
- level_rates: float32 [30, 30], replicated, may hold values from -0.6 to 0.6
Outputs:
- new_state: float32 [41, 256, 128, 128], P(None, 'mn', 'az')
The draws below stay inside these ranges and needn't reach their ends.
Inputs may be any that keep to these rules, and one draw needn't show every extreme that they name: `flow_state`: quantities 0 to 4 lie in 0.05 to 0.45 and quantity 10 in 0.5 to 2.
All inputs are finite; a program needn't handle non-finite values.
Results may differ from the reference program's by a relative error of at most 0.000098.
Values sent between devices are 32-bit elements; how exact they have to be, the bound alone decides.
A program may use at most 64 MiB of HBM per device.

```python
import jax
import jax.numpy as jnp
from jax import lax

NQ = 41
NLEV = 30
NJ = 128
NI = 256
NK = 128


def draw_flow_state(key, part):
    key = jax.random.fold_in(key, 7)
    key_dense, key_rough = jax.random.split(key, 2)
    dims = (NQ, NI, NK, NJ)
    position = jnp.arange(NQ)
    partial_value = (position < 5)[:, None, None, None]
    electron = (position == 10)[:, None, None, None]
    row_scale = jnp.where((position >= 5) & (position < 8), 2.0, 1.0).astype(jnp.float32)[:, None, None, None]
    fraction = jax.random.uniform(key_dense, dims, jnp.float32, 0.0, 1.0)
    rough = jax.random.normal(key_rough, dims, jnp.float32)
    density = 0.05 + 0.4 * fraction
    charge = 0.5 + 1.5 * fraction
    other = jnp.clip(rough * row_scale, -12.0, 12.0)
    return jnp.where(partial_value, density, jnp.where(electron, charge, other)).astype(jnp.float32)


def scatter_about(stream_key, extent, width, most, held_as=jnp.bfloat16):
    values = width * jax.random.normal(stream_key, extent, jnp.float32)
    return jnp.clip(values, min=-most, max=most).astype(held_as)


def setup_inputs(seed: int = 0) -> dict:
    key_list = jax.random.split(jax.random.key(seed), 3)
    return {
        "flow_state": draw_flow_state(jax.random.fold_in(key_list[2], 71), 0),
        "level_rates": scatter_about(key_list[1], (NLEV, NLEV), 0.1, 0.6, jnp.float32),
    }


DISSIPATION = 0.05
SOUND_SPEED = 1.0
TIME_STEP = 0.3


def pole_sign(count):
    position = jnp.arange(count)
    return jnp.where((position == 5) | (position == 7), -1.0, 1.0).astype(jnp.float32)[:, None, None, None]


def face_div(fields, velocity, axis, count):
    def window(array, offset):
        return lax.slice_in_dim(array, offset, offset + count + 1, axis=axis)
    carried = velocity * fields
    wave_speed = 0.5 * (jnp.abs(window(velocity, 1)) + jnp.abs(window(velocity, 2))) + SOUND_SPEED
    fourth = window(fields, 3) - 3.0 * window(fields, 2) + 3.0 * window(fields, 1) - window(fields, 0)
    flux = 0.5 * (window(carried, 1) + window(carried, 2)) - DISSIPATION * wave_speed * fourth
    return lax.slice_in_dim(flux, 1, count + 1, axis=axis) - lax.slice_in_dim(flux, 0, count, axis=axis)


def velocity_of(padded):
    density = jnp.sum(padded[0:5], axis=0, keepdims=True)
    return padded[5:8] / jnp.maximum(density, 1.0)


def residual(padded, velocity, level_rates):
    inner_i = padded.shape[1] - 4
    inner_k = padded.shape[2] - 4
    along_i = face_div(padded[:, :, 2:-2], velocity[0:1, :, 2:-2], 1, inner_i)
    along_k = face_div(padded[:, 2:-2], velocity[2:3, 2:-2], 2, inner_k)
    centre = padded[:, 2:-2, 2:-2]
    widths = ((0, 0), (0, 0), (0, 0), (2, 2))
    along_j = face_div(jnp.pad(centre, widths), jnp.pad(velocity[1:2, 2:-2, 2:-2], widths), 3, centre.shape[3])
    change = -(along_i + along_k + along_j)
    source = centre[10:11] * jnp.einsum('ab,bikj->aikj', level_rates, centre[11:], precision=lax.Precision.HIGHEST)
    return jnp.concatenate([change[:11], change[11:] + source], axis=0)


def ghosts(fields):
    opposite = jnp.roll(fields[:, 0:2], NK // 2, axis=2)[:, ::-1] * pole_sign(fields.shape[0])
    beyond = jnp.zeros_like(fields[:, 0:2])
    extended = jnp.concatenate([opposite, fields, beyond], axis=1)
    return jnp.concatenate([extended[:, :, -2:], extended, extended[:, :, :2]], axis=2)


def reference(flow_state, level_rates):
    padded = ghosts(flow_state)
    velocity = velocity_of(padded)
    section_one = flow_state + TIME_STEP * residual(padded, velocity, level_rates)
    second = residual(ghosts(section_one), velocity, level_rates)
    return 0.5 * flow_state + 0.5 * (section_one + TIME_STEP * second)
```

```python
import functools

import jax
import jax.numpy as jnp
from jax import lax
from jax.experimental import pallas as pl
from jax.experimental.pallas import tpu as pltpu
from jax.sharding import PartitionSpec as P

MESH = pl.DeviceIdType.MESH
DISSIPATION = 0.05
SOUND_SPEED = 1.0
TIME_STEP = 0.3
NQ, NLEV, FIRST_LEVEL, ELECTRON = 41, 30, 11, 10
ROWS, LANES = 8, 128
COLUMNS = 4
BOUNDS = (0, 11, 21, 31, 41)


def parts_of(a, b):
    cuts = [a + ((b - a) * p + COLUMNS - 1) // COLUMNS for p in range(COLUMNS + 1)]
    return [(cuts[p], cuts[p + 1]) for p in range(COLUMNS)]


CHUNKS = [(a, b, parts_of(a, b)) for a, b in zip(BOUNDS[:-1], BOUNDS[1:])]
NC = len(CHUNKS)


def as_int(flag):
    return flag.astype(jnp.int32)


def kernel(flow, rates, out, q, s1, new, coef, halo, hk, rf, rb,
           in_sem, out_sem, s_far, s_near, s_az, s_rel, r_halo, r_rel, r_az):
    mn, az = lax.axis_index("mn"), lax.axis_index("az")
    n_mn, n_az = lax.axis_size("mn"), lax.axis_size("az")
    groups = n_mn // COLUMNS
    x, m = lax.rem(mn, COLUMNS), lax.div(mn, COLUMNS)
    opp = lax.rem(az + n_az // 2, n_az)
    az_up, az_dn = lax.rem(az + 1, n_az), lax.rem(az + n_az - 1, n_az)
    pole = mn == 0
    first, last = x == 0, x == COLUMNS - 1
    up_far = last & (m < groups - 1)
    f_to = (4 * m + 4, az)
    b_to = (jnp.where(pole | (m == 0), 0, 4 * m - 1), jnp.where(m == 0, opp, az))
    b_side = jnp.where(m == 0, 0, 1)

    bar = pltpu.get_barrier_semaphore()

    def tell(cond, device):
        @pl.when(cond)
        def _():
            pl.semaphore_signal(bar, 1, device_id=device, device_id_type=MESH)

    far_az = jnp.where(pole, opp, az)
    tell(first, (jnp.where(pole, 0, mn - 1), far_az))
    for p in range(3):
        tell(first, (jnp.where(pole, p + 1, mn - 4 + p), far_az))
        tell(up_far, (mn + 2 + p, az))
    tell(up_far, (mn + 1, az))
    tell(jnp.logical_not(last) & (m < groups - 1), (4 * m + 3, az))
    tell(jnp.logical_not(first), (4 * m, az))
    tell(jnp.logical_not(first), (mn - 1, az))
    tell(jnp.logical_not(last), (mn + 1, az))
    for other in (az_up, az_dn):
        pl.semaphore_signal(bar, 1, device_id=(mn, other), device_id_type=MESH)
    targets = 2 + 4 * as_int(first) + 4 * as_int(up_far) + 2 * as_int(jnp.logical_not(first))
    targets += as_int(jnp.logical_not(last)) + as_int(jnp.logical_not(last) & (m < groups - 1))

    load = pltpu.make_async_copy(flow, q, in_sem)
    load.start()

    @pl.when(mn == n_mn - 1)
    def _():
        for e in range(2):
            halo[e, 1] = jnp.zeros((NQ, 2, ROWS, LANES), jnp.float32)

    load.wait()

    def source(field, acc):
        def pair(t, _):
            a = 2 * t
            sums = [[None] * ROWS, [None] * ROWS]
            for b in range(NLEV):
                r0, r1 = rates[a, b], rates[a + 1, b]
                for i in range(ROWS):
                    v = field[FIRST_LEVEL + b, i]
                    for s, r in ((0, r0), (1, r1)):
                        term = v * r
                        sums[s][i] = term if b == 0 else sums[s][i] + term
            for i in range(ROWS):
                scale = TIME_STEP * field[ELECTRON, i]
                for s in range(2):
                    acc[FIRST_LEVEL + a + s, i] = scale * sums[s][i]
            return 0
        lax.fori_loop(0, NLEV // 2, pair, 0)

    source(q, s1)
    pl.semaphore_wait(bar, targets)

    started = []

    def copy(src, dst, s, r, device):
        return pltpu.make_async_remote_copy(src, dst, s, r, device_id=device, device_id_type=MESH)

    def start(cond, c):
        if cond is None:
            c.start()
        else:
            pl.when(cond)(lambda: c.start())
        started.append((cond, c))

    def send_far(e, c, field):
        _, _, parts = CHUNKS[c]
        for p in range(4):
            a, b = parts[p]
            if p == 3:
                start(up_far, copy(field.at[a:b, 6:8], halo.at[e, 0, a:b], s_far.at[e, 0, c, p], r_halo.at[e, 0, c, p], f_to))
            else:
                start(up_far, copy(field.at[a:b, 6:8], rf.at[e, a:b], s_far.at[e, 0, c, p], r_rel.at[e, 0, c], (4 * m + p, az)))
            p = 3 - p
            a, b = parts[p]
            if p == 0:
                start(first, copy(field.at[a:b, 0:2], halo.at[e, b_side, a:b], s_far.at[e, 1, c, p], r_halo.at[e, b_side, c, p], b_to))
            else:
                start(first, copy(field.at[a:b, 0:2], rb.at[e, a:b], s_far.at[e, 1, c, p], r_rel.at[e, 1, c], (4 * m + p, az)))

    def send_az(e, c, field):
        a, b, _ = CHUNKS[c]
        start(None, copy(field.at[a:b, :, 0:2], hk.at[e, a:b, :, 0:2], s_az.at[e, 0, c], r_az.at[e, 0, c], (mn, az_dn)))
        start(None, copy(field.at[a:b, :, 6:8], hk.at[e, a:b, :, 6:8], s_az.at[e, 1, c], r_az.at[e, 1, c], (mn, az_up)))

    def send_near(e, c, field):
        a, b, _ = CHUNKS[c]
        start(jnp.logical_not(last), copy(field.at[a:b, 6:8], halo.at[e, 0, a:b], s_near.at[e, 0, c], r_halo.at[e, 0, c, 0], (mn + 1, az)))
        start(jnp.logical_not(first), copy(field.at[a:b, 0:2], halo.at[e, 1, a:b], s_near.at[e, 1, c], r_halo.at[e, 1, c, 0], (mn - 1, az)))

    def await_copy(cond, dst, r):
        c = copy(dst, dst, in_sem, r, f_to)
        if cond is None:
            c.wait_recv()
        else:
            pl.when(cond)(lambda: c.wait_recv())

    def relay(e, c):
        _, _, parts = CHUNKS[c]
        for p in range(4):
            a, b = parts[p]
            if p != 3:
                cond = (x == p) & (m < groups - 1)
                await_copy(cond, rf.at[e, a:b], r_rel.at[e, 0, c])
                start(cond, copy(rf.at[e, a:b], halo.at[e, 0, a:b], s_rel.at[e, 0, c], r_halo.at[e, 0, c, p], f_to))
            if p != 0:
                cond = x == p
                await_copy(cond, rb.at[e, a:b], r_rel.at[e, 1, c])
                start(cond, copy(rb.at[e, a:b], halo.at[e, b_side, a:b], s_rel.at[e, 1, c], r_halo.at[e, b_side, c, p], b_to))

    def await_margins(e, c):
        a, b, parts = CHUNKS[c]
        await_copy(None, hk.at[e, a:b, :, 0:2], r_az.at[e, 0, c])
        await_copy(None, hk.at[e, a:b, :, 6:8], r_az.at[e, 1, c])
        await_copy(jnp.logical_not(first), halo.at[e, 0, a:b], r_halo.at[e, 0, c, 0])
        await_copy(jnp.logical_not(last), halo.at[e, 1, a:b], r_halo.at[e, 1, c, 0])
        for p in range(4):
            pa, pb = parts[p]
            await_copy(first, halo.at[e, 0, pa:pb], r_halo.at[e, 0, c, p])
            await_copy(up_far, halo.at[e, 1, pa:pb], r_halo.at[e, 1, c, p])
        if c == 0:
            @pl.when(pole)
            def _():
                for n in (5, 7):
                    halo[e, 0, n] = -halo[e, 0, n]

    below = (jnp.where(pole, 0, 1), jnp.where(pole, 1, 0))

    def row(e, field, n, i):
        if i < 0:
            return halo[e, 0, n, below[-i - 1]]
        if i >= ROWS:
            return halo[e, 1, n, i - ROWS]
        return field[n, i]

    k_at = lax.broadcasted_iota(jnp.int32, (ROWS, LANES), 0)
    j_at = lax.broadcasted_iota(jnp.int32, (ROWS, LANES), 1)

    def along_k(v, h):
        return [
            pltpu.roll(jnp.where(k_at < 1, h, v), 7, 0),
            pltpu.roll(jnp.where(k_at < 2, h, v), 6, 0),
            pltpu.roll(jnp.where(k_at >= 7, h, v), 1, 0),
            pltpu.roll(jnp.where(k_at >= 6, h, v), 2, 0),
        ]

    def speed(u, v):
        return DISSIPATION * (0.5 * (jnp.abs(u) + jnp.abs(v)) + SOUND_SPEED)

    def taps(u_m, u, u_p):
        s_m, s_p = speed(u_m, u), speed(u, u_p)
        return (
            TIME_STEP * (-0.5 * u_p - 3.0 * s_p - s_m),
            TIME_STEP * s_p,
            TIME_STEP * (0.5 * u_m - s_p - 3.0 * s_m),
            TIME_STEP * s_m,
            (3.0 * TIME_STEP) * (s_p + s_m),
        )

    def coefficients():
        def density(read):
            return 1.0 / jnp.maximum(read(0) + read(1) + read(2) + read(3) + read(4), 1.0)

        def u_i(i):
            return row(0, q, 5, i) * density(lambda n: row(0, q, n, i))

        u_m, u = u_i(-1), u_i(0)
        for i in range(ROWS):
            u_p = u_i(i + 1)
            inverse = density(lambda n: q[n, i])
            ti = taps(u_m, u, u_p)
            u_m, u = u, u_p
            uk = q[7, i] * inverse
            hk_u = hk[0, 7, i] * density(lambda n: hk[0, n, i])
            shifted = along_k(uk, hk_u)
            tk = taps(shifted[2], uk, shifted[0])
            uj = q[6, i] * inverse
            uj_p = jnp.where(j_at < LANES - 1, pltpu.roll(uj, LANES - 1, 1), 0.0)
            uj_m = jnp.where(j_at > 0, pltpu.roll(uj, 1, 1), 0.0)
            tj = taps(uj_m, uj, uj_p)
            for t in range(4):
                coef[t, i] = ti[t]
                coef[4 + t, i] = tk[t]
            coef[8, i] = jnp.where(j_at < LANES - 1, tj[0], 0.0)
            coef[9, i] = jnp.where(j_at < LANES - 2, tj[1], 0.0)
            coef[10, i] = jnp.where(j_at > 0, tj[2], 0.0)
            coef[11, i] = jnp.where(j_at > 1, tj[3], 0.0)
            coef[12, i] = 1.0 + ti[4] + tk[4] + tj[4]

    def section(e, field, acc, a, b, chemistry, final):
        for i in range(ROWS):
            cs = [coef[t, i] for t in range(13)]

            def one(n, _):
                v = field[n, i]
                r = cs[12] * v
                for t, d in enumerate((1, 2, -1, -2)):
                    r = r + cs[t] * row(e, field, n, i + d)
                ks = along_k(v, hk[e, n, i])
                for t in range(4):
                    r = r + cs[4 + t] * ks[t]
                for t, d in enumerate((1, 2, -1, -2)):
                    r = r + cs[8 + t] * pltpu.roll(v, (LANES - d) % LANES, 1)
                if chemistry:
                    r = r + acc[n, i]
                acc[n, i] = 0.5 * (q[n, i] + r) if final else r
                return 0

            lax.fori_loop(a, b, one, 0)

    for c in range(NC):
        send_far(0, c, q)
    for c in range(NC):
        send_az(0, c, q)
    for c in range(NC):
        send_near(0, c, q)
    for c in range(NC):
        relay(0, c)
    for c in range(NC):
        a, b, _ = CHUNKS[c]
        await_margins(0, c)
        if c == 0:
            coefficients()
        section(0, q, s1, a, b, c > 0, False)
        send_far(1, c, s1)
        send_az(1, c, s1)
        send_near(1, c, s1)
        relay(1, c)
    source(s1, new)
    stores = []
    for c in range(NC):
        a, b, _ = CHUNKS[c]
        await_margins(1, c)
        section(1, s1, new, a, b, c > 0, True)
        store = pltpu.make_async_copy(new.at[a:b], out.at[a:b], out_sem.at[c])
        store.start()
        stores.append(store)
    for cond, c in started:
        if cond is None:
            c.wait_send()
        else:
            pl.when(cond)(lambda c=c: c.wait_send())
    for store in stores:
        store.wait()


def on_device(flow_state, level_rates):
    def vmem(*shape):
        return pltpu.VMEM(shape, jnp.float32)

    def sems(*shape):
        return pltpu.SemaphoreType.DMA(shape)

    block = (NQ, ROWS, ROWS, LANES)
    margin = (NQ, 2, ROWS, LANES)
    return pl.pallas_call(
        kernel,
        out_shape=jax.ShapeDtypeStruct(block, jnp.float32),
        in_specs=[pl.BlockSpec(memory_space=pl.ANY), pl.BlockSpec(memory_space=pltpu.SMEM)],
        out_specs=pl.BlockSpec(memory_space=pl.ANY),
        scratch_shapes=[
            vmem(*block), vmem(*block), vmem(*block), vmem(13, ROWS, ROWS, LANES),
            vmem(2, 2, *margin), vmem(2, *block), vmem(2, *margin), vmem(2, *margin),
            pltpu.SemaphoreType.DMA, sems(NC), sems(2, 2, NC, 4), sems(2, 2, NC), sems(2, 2, NC), sems(2, 2, NC),
            sems(2, 2, NC, 4), sems(2, 2, NC), sems(2, 2, NC),
        ],
        compiler_params=pltpu.CompilerParams(
            collective_id=0, has_side_effects=True, vmem_limit_bytes=40 * 1024 * 1024
        ),
    )(flow_state, level_rates)


def solution(mesh):
    in_specs = (P(None, "mn", "az", None), P())
    out_specs = P(None, "mn", "az", None)
    return jax.shard_map(
        on_device, mesh=mesh, in_specs=in_specs, out_specs=out_specs, check_vma=False
    )
```

```python
import functools

import jax
import jax.numpy as jnp
from jax import lax
from jax.experimental import pallas as pl
from jax.experimental.pallas import tpu as pltpu
from jax.sharding import PartitionSpec as P

MESH = pl.DeviceIdType.MESH
DISSIPATION = 0.05
SOUND_SPEED = 1.0
TIME_STEP = 0.3
NQ, NLEV, FIRST_LEVEL, ELECTRON = 41, 30, 11, 10
ROWS, LANES = 8, 128
COLUMNS = 4
BOUNDS = (0, 11, 21, 31, 41)
UNROLL = 10


def parts_of(a, b):
    cuts = [a + ((b - a) * p + COLUMNS - 1) // COLUMNS for p in range(COLUMNS + 1)]
    return [(cuts[p], cuts[p + 1]) for p in range(COLUMNS)]


CHUNKS = [(a, b, parts_of(a, b)) for a, b in zip(BOUNDS[:-1], BOUNDS[1:])]
NC = len(CHUNKS)


def as_int(flag):
    return flag.astype(jnp.int32)


def kernel(flow, rates, out, q, s1, new, coef, halo, hk, rf, rb,
           in_sem, out_sem, s_far, s_near, s_az, s_rel, r_halo, r_rel, r_az):
    mn, az = lax.axis_index("mn"), lax.axis_index("az")
    n_mn, n_az = lax.axis_size("mn"), lax.axis_size("az")
    groups = n_mn // COLUMNS
    x, m = lax.rem(mn, COLUMNS), lax.div(mn, COLUMNS)
    opp = lax.rem(az + n_az // 2, n_az)
    az_up, az_dn = lax.rem(az + 1, n_az), lax.rem(az + n_az - 1, n_az)
    pole = mn == 0
    first, last = x == 0, x == COLUMNS - 1
    up_far = last & (m < groups - 1)
    f_to = (4 * m + 4, az)
    b_to = (jnp.where(pole | (m == 0), 0, 4 * m - 1), jnp.where(m == 0, opp, az))
    b_side = jnp.where(m == 0, 0, 1)

    bar = pltpu.get_barrier_semaphore()

    def tell(cond, device):
        @pl.when(cond)
        def _():
            pl.semaphore_signal(bar, 1, device_id=device, device_id_type=MESH)

    far_az = jnp.where(pole, opp, az)
    tell(first, (jnp.where(pole, 0, mn - 1), far_az))
    for p in range(3):
        tell(first, (jnp.where(pole, p + 1, mn - 4 + p), far_az))
        tell(up_far, (mn + 2 + p, az))
    tell(up_far, (mn + 1, az))
    tell(jnp.logical_not(last) & (m < groups - 1), (4 * m + 3, az))
    tell(jnp.logical_not(first), (4 * m, az))
    tell(jnp.logical_not(first), (mn - 1, az))
    tell(jnp.logical_not(last), (mn + 1, az))
    for other in (az_up, az_dn):
        pl.semaphore_signal(bar, 1, device_id=(mn, other), device_id_type=MESH)
    targets = 2 + 4 * as_int(first) + 4 * as_int(up_far) + 2 * as_int(jnp.logical_not(first))
    targets += as_int(jnp.logical_not(last)) + as_int(jnp.logical_not(last) & (m < groups - 1))

    load = pltpu.make_async_copy(flow, q, in_sem)
    load.start()

    @pl.when(mn == n_mn - 1)
    def _():
        for e in range(2):
            halo[e, 1] = jnp.zeros((NQ, 2, ROWS, LANES), jnp.float32)

    load.wait()

    def source(field, acc):
        def pair(t, _):
            a = 2 * t
            sums = [[None] * ROWS, [None] * ROWS]
            for b in range(NLEV):
                r0, r1 = rates[a, b], rates[a + 1, b]
                for i in range(ROWS):
                    v = field[FIRST_LEVEL + b, i]
                    for s, r in ((0, r0), (1, r1)):
                        term = v * r
                        sums[s][i] = term if b == 0 else sums[s][i] + term
            for i in range(ROWS):
                scale = TIME_STEP * field[ELECTRON, i]
                for s in range(2):
                    acc[FIRST_LEVEL + a + s, i] = scale * sums[s][i]
            return 0
        lax.fori_loop(0, NLEV // 2, pair, 0)

    source(q, s1)
    pl.semaphore_wait(bar, targets)

    started = []

    def copy(src, dst, s, r, device):
        return pltpu.make_async_remote_copy(src, dst, s, r, device_id=device, device_id_type=MESH)

    def start(cond, c):
        if cond is None:
            c.start()
        else:
            pl.when(cond)(lambda: c.start())
        started.append((cond, c))

    def send_far(e, c, field):
        _, _, parts = CHUNKS[c]
        for p in range(4):
            a, b = parts[p]
            if p == 3:
                start(up_far, copy(field.at[a:b, 6:8], halo.at[e, 0, a:b], s_far.at[e, 0, c, p], r_halo.at[e, 0, c, p], f_to))
            else:
                start(up_far, copy(field.at[a:b, 6:8], rf.at[e, a:b], s_far.at[e, 0, c, p], r_rel.at[e, 0, c], (4 * m + p, az)))
            p = 3 - p
            a, b = parts[p]
            if p == 0:
                start(first, copy(field.at[a:b, 0:2], halo.at[e, b_side, a:b], s_far.at[e, 1, c, p], r_halo.at[e, b_side, c, p], b_to))
            else:
                start(first, copy(field.at[a:b, 0:2], rb.at[e, a:b], s_far.at[e, 1, c, p], r_rel.at[e, 1, c], (4 * m + p, az)))

    def send_az(e, c, field):
        a, b, _ = CHUNKS[c]
        start(None, copy(field.at[a:b, :, 0:2], hk.at[e, a:b, :, 0:2], s_az.at[e, 0, c], r_az.at[e, 0, c], (mn, az_dn)))
        start(None, copy(field.at[a:b, :, 6:8], hk.at[e, a:b, :, 6:8], s_az.at[e, 1, c], r_az.at[e, 1, c], (mn, az_up)))

    def send_near(e, c, field):
        a, b, _ = CHUNKS[c]
        start(jnp.logical_not(last), copy(field.at[a:b, 6:8], halo.at[e, 0, a:b], s_near.at[e, 0, c], r_halo.at[e, 0, c, 0], (mn + 1, az)))
        start(jnp.logical_not(first), copy(field.at[a:b, 0:2], halo.at[e, 1, a:b], s_near.at[e, 1, c], r_halo.at[e, 1, c, 0], (mn - 1, az)))

    def await_copy(cond, dst, r):
        c = copy(dst, dst, in_sem, r, f_to)
        if cond is None:
            c.wait_recv()
        else:
            pl.when(cond)(lambda: c.wait_recv())

    def relay(e, c):
        _, _, parts = CHUNKS[c]
        for p in range(4):
            a, b = parts[p]
            if p != 3:
                cond = (x == p) & (m < groups - 1)
                await_copy(cond, rf.at[e, a:b], r_rel.at[e, 0, c])
                start(cond, copy(rf.at[e, a:b], halo.at[e, 0, a:b], s_rel.at[e, 0, c], r_halo.at[e, 0, c, p], f_to))
            if p != 0:
                cond = x == p
                await_copy(cond, rb.at[e, a:b], r_rel.at[e, 1, c])
                start(cond, copy(rb.at[e, a:b], halo.at[e, b_side, a:b], s_rel.at[e, 1, c], r_halo.at[e, b_side, c, p], b_to))

    def await_margins(e, c):
        a, b, parts = CHUNKS[c]
        await_copy(None, hk.at[e, a:b, :, 0:2], r_az.at[e, 0, c])
        await_copy(None, hk.at[e, a:b, :, 6:8], r_az.at[e, 1, c])
        await_copy(jnp.logical_not(first), halo.at[e, 0, a:b], r_halo.at[e, 0, c, 0])
        await_copy(jnp.logical_not(last), halo.at[e, 1, a:b], r_halo.at[e, 1, c, 0])
        for p in range(4):
            pa, pb = parts[p]
            await_copy(first, halo.at[e, 0, pa:pb], r_halo.at[e, 0, c, p])
            await_copy(up_far, halo.at[e, 1, pa:pb], r_halo.at[e, 1, c, p])
        if c == 0:
            @pl.when(pole)
            def _():
                for n in (5, 7):
                    halo[e, 0, n] = -halo[e, 0, n]

    below = (jnp.where(pole, 0, 1), jnp.where(pole, 1, 0))

    def row(e, field, n, i):
        if i < 0:
            return halo[e, 0, n, below[-i - 1]]
        if i >= ROWS:
            return halo[e, 1, n, i - ROWS]
        return field[n, i]

    k_at = lax.broadcasted_iota(jnp.int32, (ROWS, LANES), 0)
    j_at = lax.broadcasted_iota(jnp.int32, (ROWS, LANES), 1)

    def along_k(v, h):
        return [
            pltpu.roll(jnp.where(k_at < 1, h, v), 7, 0),
            pltpu.roll(jnp.where(k_at < 2, h, v), 6, 0),
            pltpu.roll(jnp.where(k_at >= 7, h, v), 1, 0),
            pltpu.roll(jnp.where(k_at >= 6, h, v), 2, 0),
        ]

    def speed(u, v):
        return DISSIPATION * (0.5 * (jnp.abs(u) + jnp.abs(v)) + SOUND_SPEED)

    def taps(u_m, u, u_p):
        s_m, s_p = speed(u_m, u), speed(u, u_p)
        return (
            TIME_STEP * (-0.5 * u_p - 3.0 * s_p - s_m),
            TIME_STEP * s_p,
            TIME_STEP * (0.5 * u_m - s_p - 3.0 * s_m),
            TIME_STEP * s_m,
            (3.0 * TIME_STEP) * (s_p + s_m),
        )

    def coefficients():
        def density(read):
            return 1.0 / jnp.maximum(read(0) + read(1) + read(2) + read(3) + read(4), 1.0)

        def u_i(i):
            return row(0, q, 5, i) * density(lambda n: row(0, q, n, i))

        u_m, u = u_i(-1), u_i(0)
        for i in range(ROWS):
            u_p = u_i(i + 1)
            inverse = density(lambda n: q[n, i])
            ti = taps(u_m, u, u_p)
            u_m, u = u, u_p
            uk = q[7, i] * inverse
            hk_u = hk[0, 7, i] * density(lambda n: hk[0, n, i])
            shifted = along_k(uk, hk_u)
            tk = taps(shifted[2], uk, shifted[0])
            uj = q[6, i] * inverse
            uj_p = jnp.where(j_at < LANES - 1, pltpu.roll(uj, LANES - 1, 1), 0.0)
            uj_m = jnp.where(j_at > 0, pltpu.roll(uj, 1, 1), 0.0)
            tj = taps(uj_m, uj, uj_p)
            for t in range(4):
                coef[t, i] = ti[t]
                coef[4 + t, i] = tk[t]
            coef[8, i] = jnp.where(j_at < LANES - 1, tj[0], 0.0)
            coef[9, i] = jnp.where(j_at < LANES - 2, tj[1], 0.0)
            coef[10, i] = jnp.where(j_at > 0, tj[2], 0.0)
            coef[11, i] = jnp.where(j_at > 1, tj[3], 0.0)
            coef[12, i] = 1.0 + ti[4] + tk[4] + tj[4]

    def section(e, field, acc, a, b, chemistry, final):
        for i in range(ROWS):
            cs = [coef[t, i] for t in range(13)]

            def one(n):
                v = field[n, i]
                ks = along_k(v, hk[e, n, i])
                js = [pltpu.roll(v, (LANES - d) % LANES, 1) for d in (1, 2, -1, -2)]
                rows = [row(e, field, n, i + d) for d in (1, 2, -1, -2)]
                sums = [cs[12] * v]
                for base, values in ((0, rows), (4, ks), (8, js)):
                    t = [cs[base + d] * values[d] for d in range(4)]
                    sums.append((t[0] + t[1]) + (t[2] + t[3]))
                r = (sums[0] + sums[1]) + (sums[2] + sums[3])
                if chemistry:
                    r = r + acc[n, i]
                acc[n, i] = 0.5 * (q[n, i] + r) if final else r

            def several(g, _):
                for s in range(UNROLL):
                    one(a + g * UNROLL + s)
                return 0

            lax.fori_loop(0, (b - a) // UNROLL, several, 0)
            for n in range(a + (b - a) // UNROLL * UNROLL, b):
                one(n)

    for c in range(NC):
        send_far(0, c, q)
    for c in range(NC):
        send_az(0, c, q)
    for c in range(NC):
        send_near(0, c, q)
    for c in range(NC):
        relay(0, c)
    for c in range(NC):
        a, b, _ = CHUNKS[c]
        await_margins(0, c)
        if c == 0:
            coefficients()
        section(0, q, s1, a, b, c > 0, False)
        send_far(1, c, s1)
        send_az(1, c, s1)
        send_near(1, c, s1)
        relay(1, c)
    source(s1, new)
    stores = []
    for c in range(NC):
        a, b, _ = CHUNKS[c]
        await_margins(1, c)
        section(1, s1, new, a, b, c > 0, True)
        store = pltpu.make_async_copy(new.at[a:b], out.at[a:b], out_sem.at[c])
        store.start()
        stores.append(store)
    for cond, c in started:
        if cond is None:
            c.wait_send()
        else:
            pl.when(cond)(lambda c=c: c.wait_send())
    for store in stores:
        store.wait()


def on_device(flow_state, level_rates):
    def vmem(*shape):
        return pltpu.VMEM(shape, jnp.float32)

    def sems(*shape):
        return pltpu.SemaphoreType.DMA(shape)

    block = (NQ, ROWS, ROWS, LANES)
    margin = (NQ, 2, ROWS, LANES)
    return pl.pallas_call(
        kernel,
        out_shape=jax.ShapeDtypeStruct(block, jnp.float32),
        in_specs=[pl.BlockSpec(memory_space=pl.ANY), pl.BlockSpec(memory_space=pltpu.SMEM)],
        out_specs=pl.BlockSpec(memory_space=pl.ANY),
        scratch_shapes=[
            vmem(*block), vmem(*block), vmem(*block), vmem(13, ROWS, ROWS, LANES),
            vmem(2, 2, *margin), vmem(2, *block), vmem(2, *margin), vmem(2, *margin),
            pltpu.SemaphoreType.DMA, sems(NC), sems(2, 2, NC, 4), sems(2, 2, NC), sems(2, 2, NC), sems(2, 2, NC),
            sems(2, 2, NC, 4), sems(2, 2, NC), sems(2, 2, NC),
        ],
        compiler_params=pltpu.CompilerParams(
            collective_id=0, has_side_effects=True, vmem_limit_bytes=40 * 1024 * 1024
        ),
    )(flow_state, level_rates)


def solution(mesh):
    in_specs = (P(None, "mn", "az", None), P())
    out_specs = P(None, "mn", "az", None)
    return jax.shard_map(
        on_device, mesh=mesh, in_specs=in_specs, out_specs=out_specs, check_vma=False
    )
```

```python
import functools

import jax
import jax.numpy as jnp
from jax import lax
from jax.experimental import pallas as pl
from jax.experimental.pallas import tpu as pltpu
from jax.sharding import PartitionSpec as P

MESH = pl.DeviceIdType.MESH
DISSIPATION = 0.05
SOUND_SPEED = 1.0
TIME_STEP = 0.3
NQ, NLEV, FIRST_LEVEL, ELECTRON = 41, 30, 11, 10
ROWS, LANES = 8, 128
COLUMNS = 4
BOUNDS = (0, 11, 21, 31, 41)
UNROLL = 10
POLE_GROUP, POLE_CHUNKS = 6, (1, 3)


def parts_of(a, b):
    cuts = [a + ((b - a) * p + COLUMNS - 1) // COLUMNS for p in range(COLUMNS + 1)]
    return [(cuts[p], cuts[p + 1]) for p in range(COLUMNS)]


CHUNKS = [(a, b, parts_of(a, b)) for a, b in zip(BOUNDS[:-1], BOUNDS[1:])]
NC = len(CHUNKS)


def as_int(flag):
    return flag.astype(jnp.int32)


def kernel(flow, rates, out, q, s1, new, coef, halo, hk, rf, rb, rp,
           in_sem, out_sem, s_far, s_near, s_az, s_rel, r_halo, r_rel, r_az, far_sem, pole_sem, wrap_sem):
    mn, az = lax.axis_index("mn"), lax.axis_index("az")
    n_mn, n_az = lax.axis_size("mn"), lax.axis_size("az")
    groups = n_mn // COLUMNS
    x, m = lax.rem(mn, COLUMNS), lax.div(mn, COLUMNS)
    opp = lax.rem(az + n_az // 2, n_az)
    az_up, az_dn = lax.rem(az + 1, n_az), lax.rem(az + n_az - 1, n_az)
    pole = mn == 0
    first, last = x == 0, x == COLUMNS - 1
    up_far = last & (m < groups - 1)
    f_to = (4 * m + 4, az)
    b_to = (jnp.where(pole | (m == 0), 0, 4 * m - 1), jnp.where(m == 0, opp, az))
    b_side = jnp.where(m == 0, 0, 1)

    even, odd = lax.rem(m, 2) == 0, lax.rem(m, 2) == 1
    g0, g6 = m == 0, m == POLE_GROUP
    low_z, high_z = az < n_az // 2, az >= n_az // 2
    above = m < groups - 1
    bar = pltpu.get_barrier_semaphore()

    def tell(cond, device, sem=bar):
        def signal():
            pl.semaphore_signal(sem, 1, device_id=device, device_id_type=MESH)
        if cond is None:
            signal()
        else:
            pl.when(cond)(signal)

    for d in range(1, 4):
        tell(None, (4 * m + lax.rem(x + d, 4), az))
    tell(None, (mn, az_dn))
    tell(az < n_az - 1, (mn, az_up))
    tell(even, (4 * m + 4, az))
    tell(even & (m > 0), (4 * m - 1, az))
    for p in range(3):
        tell(even & first & (m > 0), (4 * m - 4 + p, az))
        tell(even & last, (4 * m + 5 + p, az))
        tell(pole & low_z, (p + 1, opp))
    tell((g0 | g6) & low_z, (0, opp))
    for p in range(4):
        tell(pole & low_z, (4 * POLE_GROUP + p, opp))
    tell(g6, (0, az))
    targets = 5 - as_int(az == 0) + 4 * as_int(pole) + as_int(odd) + 3 * as_int(odd & first)
    targets += as_int(odd & above) + 3 * as_int(odd & above & last)
    targets += 8 * as_int(pole & high_z) + as_int(((g0 & (x > 0)) | g6) & high_z)

    load = pltpu.make_async_copy(flow, q, in_sem)
    load.start()

    @pl.when(mn == n_mn - 1)
    def _():
        for e in range(2):
            halo[e, 1] = jnp.zeros((NQ, 2, ROWS, LANES), jnp.float32)

    load.wait()

    def source(field, acc):
        def pair(t, _):
            a = 2 * t
            sums = [[None] * ROWS, [None] * ROWS]
            for b in range(NLEV):
                r0, r1 = rates[a, b], rates[a + 1, b]
                for i in range(ROWS):
                    v = field[FIRST_LEVEL + b, i]
                    for s, r in ((0, r0), (1, r1)):
                        term = v * r
                        sums[s][i] = term if b == 0 else sums[s][i] + term
            for i in range(ROWS):
                scale = TIME_STEP * field[ELECTRON, i]
                for s in range(2):
                    acc[FIRST_LEVEL + a + s, i] = scale * sums[s][i]
            return 0
        lax.fori_loop(0, NLEV // 2, pair, 0)

    pl.semaphore_wait(bar, targets)
    for p in range(4):
        tell(odd & first, (4 * m - 4 + p, az), far_sem)
        tell(odd & last & above, (4 * m + 4 + p, az), far_sem)
        tell(pole & high_z, (p, opp), pole_sem)
        tell(pole & high_z, (4 * POLE_GROUP + p, opp), pole_sem)
    tell(az == n_az - 1, (mn, az_up), wrap_sem)

    started = []

    def copy(src, dst, s, r, device):
        return pltpu.make_async_remote_copy(src, dst, s, r, device_id=device, device_id_type=MESH)

    def start(cond, c):
        if cond is None:
            c.start()
        else:
            pl.when(cond)(lambda: c.start())
        started.append((cond, c))

    def send_to_relays(e, c, field):
        _, _, parts = CHUNKS[c]
        for p, (a, b) in enumerate(parts):
            if p != 3:
                start(up_far, copy(field.at[a:b, 6:8], rf.at[e, a:b], s_far.at[e, 0, c, p], r_rel.at[e, 0, c], (4 * m + p, az)))
            if p != 0:
                cond = first & (m > 0) if c in POLE_CHUNKS else first
                start(cond, copy(field.at[a:b, 0:2], rb.at[e, a:b], s_far.at[e, 1, c, p], r_rel.at[e, 1, c], (4 * m + p, az)))
            if c in POLE_CHUNKS:
                start(pole, copy(field.at[a:b, 0:2], rp.at[e, a:b], s_far.at[e, 2, c, p], r_rel.at[e, 2, c], (4 * POLE_GROUP + p, az)))

    def send_direct(e, c, field, across):
        _, _, parts = CHUNKS[c]
        a, b = parts[3]
        if not across:
            start(up_far, copy(field.at[a:b, 6:8], halo.at[e, 0, a:b], s_far.at[e, 0, c, 3], r_halo.at[e, 0, c, 3], f_to))
        a, b = parts[0]
        if not across or c not in POLE_CHUNKS:
            cond = pole if across else first & (m > 0)
            start(cond, copy(field.at[a:b, 0:2], halo.at[e, b_side, a:b], s_far.at[e, 1, c, 0], r_halo.at[e, b_side, c, 0], b_to))

    def az_copies(e, c, field):
        a, b, _ = CHUNKS[c]
        return (
            copy(field.at[a:b, :, 0:2], hk.at[e, a:b, :, 0:2], s_az.at[e, 0, c], r_az.at[e, 0, c], (mn, az_dn)),
            copy(field.at[a:b, :, 6:8], hk.at[e, a:b, :, 6:8], s_az.at[e, 1, c], r_az.at[e, 1, c], (mn, az_up)),
        )

    def send_az(e, c, field):
        for one in az_copies(e, c, field):
            start(None, one)

    def send_near(e, c, field):
        a, b, _ = CHUNKS[c]
        start(jnp.logical_not(last), copy(field.at[a:b, 6:8], halo.at[e, 0, a:b], s_near.at[e, 0, c], r_halo.at[e, 0, c, 0], (mn + 1, az)))
        start(jnp.logical_not(first), copy(field.at[a:b, 0:2], halo.at[e, 1, a:b], s_near.at[e, 1, c], r_halo.at[e, 1, c, 0], (mn - 1, az)))

    def await_copy(cond, dst, r):
        c = copy(dst, dst, in_sem, r, f_to)
        if cond is None:
            c.wait_recv()
        else:
            pl.when(cond)(lambda: c.wait_recv())

    def relay(e, c, across):
        _, _, parts = CHUNKS[c]
        for p, (a, b) in enumerate(parts):
            if p != 3 and not across:
                cond = (x == p) & above
                await_copy(cond, rf.at[e, a:b], r_rel.at[e, 0, c])
                start(cond, copy(rf.at[e, a:b], halo.at[e, 0, a:b], s_rel.at[e, 0, c], r_halo.at[e, 0, c, p], f_to))
            if p != 0 and not (across and c in POLE_CHUNKS):
                cond = (x == p) & (g0 if across else m > 0)
                await_copy(cond, rb.at[e, a:b], r_rel.at[e, 1, c])
                start(cond, copy(rb.at[e, a:b], halo.at[e, b_side, a:b], s_rel.at[e, 1, c], r_halo.at[e, b_side, c, p], b_to))
            if across and c in POLE_CHUNKS:
                cond = (x == p) & g6
                await_copy(cond, rp.at[e, a:b], r_rel.at[e, 2, c])
                start(cond, copy(rp.at[e, a:b], halo.at[e, 0, a:b], s_rel.at[e, 2, c], r_halo.at[e, 0, c, p], (0, opp)))

    def await_margins(e, c):
        a, b, parts = CHUNKS[c]
        await_copy(None, hk.at[e, a:b, :, 0:2], r_az.at[e, 0, c])
        await_copy(None, hk.at[e, a:b, :, 6:8], r_az.at[e, 1, c])
        await_copy(jnp.logical_not(first), halo.at[e, 0, a:b], r_halo.at[e, 0, c, 0])
        await_copy(jnp.logical_not(last), halo.at[e, 1, a:b], r_halo.at[e, 1, c, 0])
        for p in range(4):
            pa, pb = parts[p]
            await_copy(first, halo.at[e, 0, pa:pb], r_halo.at[e, 0, c, p])
            await_copy(up_far, halo.at[e, 1, pa:pb], r_halo.at[e, 1, c, p])
        if c == 0:
            @pl.when(pole)
            def _():
                for n in (5, 7):
                    halo[e, 0, n] = -halo[e, 0, n]

    below = (jnp.where(pole, 0, 1), jnp.where(pole, 1, 0))

    def row(e, field, n, i):
        if i < 0:
            return halo[e, 0, n, below[-i - 1]]
        if i >= ROWS:
            return halo[e, 1, n, i - ROWS]
        return field[n, i]

    k_at = lax.broadcasted_iota(jnp.int32, (ROWS, LANES), 0)
    j_at = lax.broadcasted_iota(jnp.int32, (ROWS, LANES), 1)

    def along_k(v, h):
        return [
            pltpu.roll(jnp.where(k_at < 1, h, v), 7, 0),
            pltpu.roll(jnp.where(k_at < 2, h, v), 6, 0),
            pltpu.roll(jnp.where(k_at >= 7, h, v), 1, 0),
            pltpu.roll(jnp.where(k_at >= 6, h, v), 2, 0),
        ]

    def speed(u, v):
        return DISSIPATION * (0.5 * (jnp.abs(u) + jnp.abs(v)) + SOUND_SPEED)

    def taps(u_m, u, u_p):
        s_m, s_p = speed(u_m, u), speed(u, u_p)
        return (
            TIME_STEP * (-0.5 * u_p - 3.0 * s_p - s_m),
            TIME_STEP * s_p,
            TIME_STEP * (0.5 * u_m - s_p - 3.0 * s_m),
            TIME_STEP * s_m,
            (3.0 * TIME_STEP) * (s_p + s_m),
        )

    def coefficients():
        def density(read):
            return 1.0 / jnp.maximum(read(0) + read(1) + read(2) + read(3) + read(4), 1.0)

        def u_i(i):
            return row(0, q, 5, i) * density(lambda n: row(0, q, n, i))

        u_m, u = u_i(-1), u_i(0)
        for i in range(ROWS):
            u_p = u_i(i + 1)
            inverse = density(lambda n: q[n, i])
            ti = taps(u_m, u, u_p)
            u_m, u = u, u_p
            uk = q[7, i] * inverse
            hk_u = hk[0, 7, i] * density(lambda n: hk[0, n, i])
            shifted = along_k(uk, hk_u)
            tk = taps(shifted[2], uk, shifted[0])
            uj = q[6, i] * inverse
            uj_p = jnp.where(j_at < LANES - 1, pltpu.roll(uj, LANES - 1, 1), 0.0)
            uj_m = jnp.where(j_at > 0, pltpu.roll(uj, 1, 1), 0.0)
            tj = taps(uj_m, uj, uj_p)
            for t in range(4):
                coef[t, i] = ti[t]
                coef[4 + t, i] = tk[t]
            coef[8, i] = jnp.where(j_at < LANES - 1, tj[0], 0.0)
            coef[9, i] = jnp.where(j_at < LANES - 2, tj[1], 0.0)
            coef[10, i] = jnp.where(j_at > 0, tj[2], 0.0)
            coef[11, i] = jnp.where(j_at > 1, tj[3], 0.0)
            coef[12, i] = 1.0 + ti[4] + tk[4] + tj[4]

    def section(e, field, acc, a, b, chemistry, final):
        for i in range(ROWS):
            cs = [coef[t, i] for t in range(13)]

            def one(n):
                v = field[n, i]
                ks = along_k(v, hk[e, n, i])
                js = [pltpu.roll(v, (LANES - d) % LANES, 1) for d in (1, 2, -1, -2)]
                rows = [row(e, field, n, i + d) for d in (1, 2, -1, -2)]
                sums = [cs[12] * v]
                for base, values in ((0, rows), (4, ks), (8, js)):
                    t = [cs[base + d] * values[d] for d in range(4)]
                    sums.append((t[0] + t[1]) + (t[2] + t[3]))
                r = (sums[0] + sums[1]) + (sums[2] + sums[3])
                if chemistry:
                    r = r + acc[n, i]
                acc[n, i] = 0.5 * (q[n, i] + r) if final else r

            def several(g, _):
                for s in range(UNROLL):
                    one(a + g * UNROLL + s)
                return 0

            lax.fori_loop(0, (b - a) // UNROLL, several, 0)
            for n in range(a + (b - a) // UNROLL * UNROLL, b):
                one(n)

    for c in range(NC):
        send_to_relays(0, c, q)
    for c in range(NC):
        down, up = az_copies(0, c, q)
        start(az > 0, down)
        start(None, up)
    for c in range(NC):
        send_near(0, c, q)
    source(q, s1)

    @pl.when((g0 | g6) & low_z)
    def _():
        pl.semaphore_wait(pole_sem, 1)

    for c in range(NC):
        send_direct(0, c, q, True)
    for c in range(NC):
        relay(0, c, True)

    @pl.when(az == 0)
    def _():
        pl.semaphore_wait(wrap_sem, 1)

    for c in range(NC):
        start(az == 0, az_copies(0, c, q)[0])

    @pl.when(even)
    def _():
        pl.semaphore_wait(far_sem, 1 + as_int(m > 0))

    for c in range(NC):
        send_direct(0, c, q, False)
    for c in range(NC):
        relay(0, c, False)
    for c in range(NC):
        a, b, _ = CHUNKS[c]
        await_margins(0, c)
        if c == 0:
            coefficients()
        section(0, q, s1, a, b, c > 0, False)
        send_to_relays(1, c, s1)
        send_direct(1, c, s1, True)
        send_direct(1, c, s1, False)
        send_az(1, c, s1)
        send_near(1, c, s1)
        relay(1, c, True)
        relay(1, c, False)
    source(s1, new)
    stores = []
    for c in range(NC):
        a, b, _ = CHUNKS[c]
        await_margins(1, c)
        section(1, s1, new, a, b, c > 0, True)
        store = pltpu.make_async_copy(new.at[a:b], out.at[a:b], out_sem.at[c])
        store.start()
        stores.append(store)
    for cond, c in started:
        if cond is None:
            c.wait_send()
        else:
            pl.when(cond)(lambda c=c: c.wait_send())
    for store in stores:
        store.wait()


def on_device(flow_state, level_rates):
    def vmem(*shape):
        return pltpu.VMEM(shape, jnp.float32)

    def sems(*shape):
        return pltpu.SemaphoreType.DMA(shape)

    block = (NQ, ROWS, ROWS, LANES)
    margin = (NQ, 2, ROWS, LANES)
    return pl.pallas_call(
        kernel,
        out_shape=jax.ShapeDtypeStruct(block, jnp.float32),
        in_specs=[pl.BlockSpec(memory_space=pl.ANY), pl.BlockSpec(memory_space=pltpu.SMEM)],
        out_specs=pl.BlockSpec(memory_space=pl.ANY),
        scratch_shapes=[
            vmem(*block), vmem(*block), vmem(*block), vmem(13, ROWS, ROWS, LANES),
            vmem(2, 2, *margin), vmem(2, *block), vmem(2, *margin), vmem(2, *margin), vmem(2, *margin),
            pltpu.SemaphoreType.DMA, sems(NC), sems(2, 3, NC, 4), sems(2, 2, NC), sems(2, 2, NC), sems(2, 3, NC),
            sems(2, 2, NC, 4), sems(2, 3, NC), sems(2, 2, NC),
            pltpu.SemaphoreType.REGULAR, pltpu.SemaphoreType.REGULAR, pltpu.SemaphoreType.REGULAR,
        ],
        compiler_params=pltpu.CompilerParams(
            collective_id=0, has_side_effects=True, vmem_limit_bytes=40 * 1024 * 1024
        ),
    )(flow_state, level_rates)


def solution(mesh):
    in_specs = (P(None, "mn", "az", None), P())
    out_specs = P(None, "mn", "az", None)
    return jax.shard_map(
        on_device, mesh=mesh, in_specs=in_specs, out_specs=out_specs, check_vma=False
    )
```

```python
import functools

import jax
import jax.numpy as jnp
from jax import lax
from jax.experimental import pallas as pl
from jax.experimental.pallas import tpu as pltpu
from jax.sharding import PartitionSpec as P

MESH = pl.DeviceIdType.MESH
DISSIPATION = 0.05
SOUND_SPEED = 1.0
TIME_STEP = 0.3
NQ, NLEV, FIRST_LEVEL, ELECTRON = 41, 30, 11, 10
ROWS, LANES = 8, 128
COLUMNS = 4
VMEM_LIMIT = 40 * 1024 * 1024
SIZES = ((3, 3, 3, 2), (4, 3, 4, 4), (3, 4, 4, 4))
LAG = 1
POLE_GROUP, POLE_CHUNKS = 6, (0, 2)


def cuts(start, sizes):
    bounds = [start + sum(sizes[:p]) for p in range(COLUMNS + 1)]
    return bounds[0], bounds[-1], list(zip(bounds[:-1], bounds[1:]))


NC = len(SIZES)
CHUNKS = [cuts(sum(sum(sizes) for sizes in SIZES[:c]), SIZES[c]) for c in range(NC)]


def as_int(flag):
    return flag.astype(jnp.int32)


def kernel(flow, rates, out, q, s1, new, coef, halo, hk, rf, rb, rp,
           in_sem, out_sem, s_far, s_near, s_az, s_rel, r_halo, r_rel, r_az, far_sem, pole_sem, wrap_sem):
    mn, az = lax.axis_index("mn"), lax.axis_index("az")
    n_mn, n_az = lax.axis_size("mn"), lax.axis_size("az")
    groups = n_mn // COLUMNS
    x, m = lax.rem(mn, COLUMNS), lax.div(mn, COLUMNS)
    opp = lax.rem(az + n_az // 2, n_az)
    az_up, az_dn = lax.rem(az + 1, n_az), lax.rem(az + n_az - 1, n_az)
    pole = mn == 0
    first, last = x == 0, x == COLUMNS - 1
    up_far = last & (m < groups - 1)
    f_to = (4 * m + 4, az)
    b_to = (jnp.where(pole | (m == 0), 0, 4 * m - 1), jnp.where(m == 0, opp, az))
    b_side = jnp.where(m == 0, 0, 1)

    even, odd = lax.rem(m, 2) == 0, lax.rem(m, 2) == 1
    g0, g6 = m == 0, m == POLE_GROUP
    low_z, high_z = az < n_az // 2, az >= n_az // 2
    above = m < groups - 1
    not_first, not_last = jnp.logical_not(first), jnp.logical_not(last)
    back, back_or_pole = first & (m > 0), first
    wrap_dn, no_wrap_dn = az == 0, az > 0
    relays_f = [(x == p) & above for p in range(4)]
    relays_b = [(x == p) & (m > 0) for p in range(4)]
    relays_0 = [(x == p) & g0 for p in range(4)]
    relays_6 = [(x == p) & g6 for p in range(4)]
    bar = pltpu.get_barrier_semaphore()

    def tell(cond, device, sem=bar):
        def signal():
            pl.semaphore_signal(sem, 1, device_id=device, device_id_type=MESH)
        if cond is None:
            signal()
        else:
            pl.when(cond)(signal)

    for d in range(1, 4):
        tell(None, (4 * m + lax.rem(x + d, 4), az))
    tell(None, (mn, az_dn))
    tell(az < n_az - 1, (mn, az_up))
    tell(even, (4 * m + 4, az))
    tell(even & (m > 0), (4 * m - 1, az))
    for p in range(3):
        tell(even & first & (m > 0), (4 * m - 4 + p, az))
        tell(even & last, (4 * m + 5 + p, az))
        tell(pole & low_z, (p + 1, opp))
    tell((g0 | g6) & low_z, (0, opp))
    for p in range(4):
        tell(pole & low_z, (4 * POLE_GROUP + p, opp))
    tell(g6, (0, az))
    targets = 5 - as_int(az == 0) + 4 * as_int(pole) + as_int(odd) + 3 * as_int(odd & first)
    targets += as_int(odd & above) + 3 * as_int(odd & above & last)
    targets += 8 * as_int(pole & high_z) + as_int(((g0 & (x > 0)) | g6) & high_z)

    load = pltpu.make_async_copy(flow, q, in_sem)
    load.start()

    @pl.when(mn == n_mn - 1)
    def _():
        for e in range(2):
            halo[e, 1] = jnp.zeros((NQ, 2, ROWS, LANES), jnp.float32)

    load.wait()

    def source(field, acc):
        def pair(t, _):
            a = 2 * t
            sums = [[None] * ROWS, [None] * ROWS]
            for b in range(NLEV):
                r0, r1 = rates[a, b], rates[a + 1, b]
                for i in range(ROWS):
                    v = field[FIRST_LEVEL + b, i]
                    for s, r in ((0, r0), (1, r1)):
                        term = v * r
                        sums[s][i] = term if b == 0 else sums[s][i] + term
            for i in range(ROWS):
                scale = TIME_STEP * field[ELECTRON, i]
                for s in range(2):
                    acc[FIRST_LEVEL + a + s, i] = scale * sums[s][i]
            return 0
        lax.fori_loop(0, NLEV // 2, pair, 0)

    pl.semaphore_wait(bar, targets)
    for p in range(4):
        tell(odd & first, (4 * m - 4 + p, az), far_sem)
        tell(odd & last & above, (4 * m + 4 + p, az), far_sem)
        tell(pole & high_z, (p, opp), pole_sem)
        tell(pole & high_z, (4 * POLE_GROUP + p, opp), pole_sem)
    tell(az == n_az - 1, (mn, az_up), wrap_sem)

    started = []

    def copy(src, dst, s, r, device):
        return pltpu.make_async_remote_copy(src, dst, s, r, device_id=device, device_id_type=MESH)

    def start(cond, *copies):
        def go():
            for c in copies:
                c.start()
        if cond is None:
            go()
        else:
            pl.when(cond)(go)
        started.append((cond, copies))

    def send_to_relays(e, c, field):
        _, _, parts = CHUNKS[c]

        def handed(side, rows, to, p, group):
            a, b = parts[p]
            return copy(field.at[a:b, rows:rows + 2], to.at[e, a:b], s_far.at[e, side, c, p], r_rel.at[e, side, c], (4 * group + p, az))

        start(up_far, *[handed(0, 6, rf, p, m) for p in range(3)])
        start(back if c in POLE_CHUNKS else back_or_pole, *[handed(1, 0, rb, p, m) for p in range(1, 4)])
        if c in POLE_CHUNKS:
            start(pole, *[handed(2, 0, rp, p, POLE_GROUP) for p in range(4)])

    def send_direct(e, c, field, across):
        _, _, parts = CHUNKS[c]
        a, b = parts[3]
        if not across:
            start(up_far, copy(field.at[a:b, 6:8], halo.at[e, 0, a:b], s_far.at[e, 0, c, 3], r_halo.at[e, 0, c, 3], f_to))
        a, b = parts[0]
        if not across or c not in POLE_CHUNKS:
            cond = pole if across else back
            start(cond, copy(field.at[a:b, 0:2], halo.at[e, b_side, a:b], s_far.at[e, 1, c, 0], r_halo.at[e, b_side, c, 0], b_to))

    def az_copies(e, c, field):
        a, b, _ = CHUNKS[c]
        return (
            copy(field.at[a:b, :, 0:2], hk.at[e, a:b, :, 0:2], s_az.at[e, 0, c], r_az.at[e, 0, c], (mn, az_dn)),
            copy(field.at[a:b, :, 6:8], hk.at[e, a:b, :, 6:8], s_az.at[e, 1, c], r_az.at[e, 1, c], (mn, az_up)),
        )

    def send_az(e, c, field):
        start(None, *az_copies(e, c, field))

    def send_near(e, c, field):
        a, b, _ = CHUNKS[c]
        start(not_last, copy(field.at[a:b, 6:8], halo.at[e, 0, a:b], s_near.at[e, 0, c], r_halo.at[e, 0, c, 0], (mn + 1, az)))
        start(not_first, copy(field.at[a:b, 0:2], halo.at[e, 1, a:b], s_near.at[e, 1, c], r_halo.at[e, 1, c, 0], (mn - 1, az)))

    def await_copies(cond, *landed):
        def go():
            for dst, r in landed:
                copy(dst, dst, in_sem, r, f_to).wait_recv()
        if cond is None:
            go()
        else:
            pl.when(cond)(go)

    def relay(e, c, across):
        _, _, parts = CHUNKS[c]

        def passed_on(cond, held, side, to, p, device):
            a, b = parts[p]
            await_copies(cond, (held.at[e, a:b], r_rel.at[e, side, c]))
            start(cond, copy(held.at[e, a:b], halo.at[e, to, a:b], s_rel.at[e, side, c], r_halo.at[e, to, c, p], device))

        for p in range(4):
            if p != 3 and not across:
                passed_on(relays_f[p], rf, 0, 0, p, f_to)
            if p != 0 and not (across and c in POLE_CHUNKS):
                passed_on((relays_0 if across else relays_b)[p], rb, 1, b_side, p, b_to)
            if across and c in POLE_CHUNKS:
                passed_on(relays_6[p], rp, 2, 0, p, (0, opp))

    def await_margins(e, c):
        a, b, parts = CHUNKS[c]
        await_copies(None, (hk.at[e, a:b, :, 0:2], r_az.at[e, 0, c]), (hk.at[e, a:b, :, 6:8], r_az.at[e, 1, c]))
        await_copies(not_first, (halo.at[e, 0, a:b], r_halo.at[e, 0, c, 0]))
        await_copies(not_last, (halo.at[e, 1, a:b], r_halo.at[e, 1, c, 0]))
        for cond, side in ((first, 0), (up_far, 1)):
            await_copies(cond, *[(halo.at[e, side, pa:pb], r_halo.at[e, side, c, p]) for p, (pa, pb) in enumerate(parts)])
        if c == 0:
            @pl.when(pole)
            def _():
                for n in (5, 7):
                    halo[e, 0, n] = -halo[e, 0, n]

    below = (jnp.where(pole, 0, 1), jnp.where(pole, 1, 0))

    def row(e, field, n, i):
        if i < 0:
            return halo[e, 0, n, below[-i - 1]]
        if i >= ROWS:
            return halo[e, 1, n, i - ROWS]
        return field[n, i]

    k_at = lax.broadcasted_iota(jnp.int32, (ROWS, LANES), 0)
    j_at = lax.broadcasted_iota(jnp.int32, (ROWS, LANES), 1)

    def along_k(v, h):
        return [
            pltpu.roll(jnp.where(k_at < 1, h, v), 7, 0),
            pltpu.roll(jnp.where(k_at < 2, h, v), 6, 0),
            pltpu.roll(jnp.where(k_at >= 7, h, v), 1, 0),
            pltpu.roll(jnp.where(k_at >= 6, h, v), 2, 0),
        ]

    def speed(u, v):
        return DISSIPATION * (0.5 * (jnp.abs(u) + jnp.abs(v)) + SOUND_SPEED)

    def taps(u_m, u, u_p):
        s_m, s_p = speed(u_m, u), speed(u, u_p)
        return (
            TIME_STEP * (-0.5 * u_p - 3.0 * s_p - s_m),
            TIME_STEP * s_p,
            TIME_STEP * (0.5 * u_m - s_p - 3.0 * s_m),
            TIME_STEP * s_m,
            (3.0 * TIME_STEP) * (s_p + s_m),
        )

    def coefficients():
        def density(read):
            return 1.0 / jnp.maximum(read(0) + read(1) + read(2) + read(3) + read(4), 1.0)

        def u_i(i):
            return row(0, q, 5, i) * density(lambda n: row(0, q, n, i))

        u_m, u = u_i(-1), u_i(0)
        for i in range(ROWS):
            u_p = u_i(i + 1)
            inverse = density(lambda n: q[n, i])
            ti = taps(u_m, u, u_p)
            u_m, u = u, u_p
            uk = q[7, i] * inverse
            hk_u = hk[0, 7, i] * density(lambda n: hk[0, n, i])
            shifted = along_k(uk, hk_u)
            tk = taps(shifted[2], uk, shifted[0])
            uj = q[6, i] * inverse
            uj_p = jnp.where(j_at < LANES - 1, pltpu.roll(uj, LANES - 1, 1), 0.0)
            uj_m = jnp.where(j_at > 0, pltpu.roll(uj, 1, 1), 0.0)
            tj = taps(uj_m, uj, uj_p)
            for t in range(4):
                coef[t, i] = ti[t]
                coef[4 + t, i] = tk[t]
            coef[8, i] = jnp.where(j_at < LANES - 1, tj[0], 0.0)
            coef[9, i] = jnp.where(j_at < LANES - 2, tj[1], 0.0)
            coef[10, i] = jnp.where(j_at > 0, tj[2], 0.0)
            coef[11, i] = jnp.where(j_at > 1, tj[3], 0.0)
            coef[12, i] = 1.0 + ti[4] + tk[4] + tj[4]

    def section(e, field, acc, a, b, chemistry, final):
        for i in range(ROWS):
            cs = [coef[t, i] for t in range(13)]

            def one(n):
                v = field[n, i]
                ks = along_k(v, hk[e, n, i])
                js = [pltpu.roll(v, (LANES - d) % LANES, 1) for d in (1, 2, -1, -2)]
                rows = [row(e, field, n, i + d) for d in (1, 2, -1, -2)]
                sums = [cs[12] * v]
                for base, values in ((0, rows), (4, ks), (8, js)):
                    t = [cs[base + d] * values[d] for d in range(4)]
                    sums.append((t[0] + t[1]) + (t[2] + t[3]))
                r = (sums[0] + sums[1]) + (sums[2] + sums[3])
                if chemistry:
                    r = r + acc[n, i]
                acc[n, i] = 0.5 * r if final else r

            for n in range(a, b):
                one(n)

    for c in range(NC):
        send_to_relays(0, c, q)
    for c in range(NC):
        down, up = az_copies(0, c, q)
        start(no_wrap_dn, down)
        start(None, up)
    for c in range(NC):
        send_near(0, c, q)
    source(q, s1)

    @pl.when((g0 | g6) & low_z)
    def _():
        pl.semaphore_wait(pole_sem, 1)

    for c in range(NC):
        send_direct(0, c, q, True)
    for c in range(NC):
        relay(0, c, True)

    @pl.when(az == 0)
    def _():
        pl.semaphore_wait(wrap_sem, 1)

    for c in range(NC):
        start(wrap_dn, az_copies(0, c, q)[0])

    @pl.when(even)
    def _():
        pl.semaphore_wait(far_sem, 1 + as_int(m > 0))

    for c in range(NC):
        send_direct(0, c, q, False)
    for c in range(NC):
        relay(0, c, False)
    for c in range(NC):
        a, b, _ = CHUNKS[c]
        await_margins(0, c)
        if c == 0:
            coefficients()
        section(0, q, s1, a, b, c > 0, False)
        send_to_relays(1, c, s1)
        send_direct(1, c, s1, True)
        send_direct(1, c, s1, False)
        send_az(1, c, s1)
        send_near(1, c, s1)
        if c >= LAG:
            relay(1, c - LAG, True)
            relay(1, c - LAG, False)
    for c in range(NC - LAG, NC):
        relay(1, c, True)
        relay(1, c, False)
    source(s1, new)
    stores = []
    for c in range(NC):
        a, b, _ = CHUNKS[c]
        await_margins(1, c)
        section(1, s1, new, a, b, c > 0, True)
        store = pltpu.make_async_copy(new.at[a:b], out.at[a:b], out_sem.at[c])
        store.start()
        stores.append(store)
    groups_of = {}
    for cond, copies in started:
        groups_of.setdefault(id(cond), (cond, []))[1].extend(copies)
    for cond, copies in groups_of.values():
        def go(copies=copies):
            for c in copies:
                c.wait_send()
        if cond is None:
            go()
        else:
            pl.when(cond)(go)
    for store in stores:
        store.wait()


def on_device(flow_state, level_rates):
    def vmem(*shape):
        return pltpu.VMEM(shape, jnp.float32)

    def sems(*shape):
        return pltpu.SemaphoreType.DMA(shape)

    block = (NQ, ROWS, ROWS, LANES)
    margin = (NQ, 2, ROWS, LANES)
    half = pl.pallas_call(
        kernel,
        out_shape=jax.ShapeDtypeStruct(block, jnp.float32),
        in_specs=[pl.BlockSpec(memory_space=pl.ANY), pl.BlockSpec(memory_space=pltpu.SMEM)],
        out_specs=pl.BlockSpec(memory_space=pl.ANY),
        scratch_shapes=[
            vmem(*block), vmem(*block), vmem(*block), vmem(13, ROWS, ROWS, LANES),
            vmem(2, 2, *margin), vmem(2, *block), vmem(2, *margin), vmem(2, *margin), vmem(2, *margin),
            pltpu.SemaphoreType.DMA, sems(NC), sems(2, 3, NC, 4), sems(2, 2, NC), sems(2, 2, NC), sems(2, 3, NC),
            sems(2, 2, NC, 4), sems(2, 3, NC), sems(2, 2, NC),
            pltpu.SemaphoreType.REGULAR, pltpu.SemaphoreType.REGULAR, pltpu.SemaphoreType.REGULAR,
        ],
        compiler_params=pltpu.CompilerParams(
            collective_id=0, has_side_effects=True, vmem_limit_bytes=VMEM_LIMIT
        ),
    )(flow_state, level_rates)
    return 0.5 * flow_state + half


def solution(mesh):
    in_specs = (P(None, "mn", "az", None), P())
    out_specs = P(None, "mn", "az", None)
    return jax.shard_map(
        on_device, mesh=mesh, in_specs=in_specs, out_specs=out_specs, check_vma=False
    )
```

```python
import functools

import jax
import jax.numpy as jnp
from jax import lax
from jax.experimental import pallas as pl
from jax.experimental.pallas import tpu as pltpu
from jax.sharding import PartitionSpec as P

MESH = pl.DeviceIdType.MESH
DISSIPATION = 0.05
SOUND_SPEED = 1.0
TIME_STEP = 0.3
NQ, NLEV, FIRST_LEVEL, ELECTRON = 41, 30, 11, 10
ROWS, LANES = 8, 128
COLUMNS = 4
VMEM_LIMIT = 60 * 1024 * 1024
UP_SIZES = ((3, 3, 3, 2), (4, 3, 4, 4), (3, 4, 4, 4))
DOWN_SIZES = ((3, 3, 3, 2), (3, 4, 4, 4), (4, 4, 3, 4))
LAG = 1
POLE_GROUP, POLE_CHUNKS = 6, (0, 2)


def cuts(start, sizes):
    bounds = [start + sum(sizes[:p]) for p in range(COLUMNS + 1)]
    return bounds[0], bounds[-1], list(zip(bounds[:-1], bounds[1:]))


NC = len(UP_SIZES)
STARTS = [sum(sum(sizes) for sizes in UP_SIZES[:c]) for c in range(NC)]
CHUNKS = [(*cuts(STARTS[c], UP_SIZES[c]), cuts(STARTS[c], DOWN_SIZES[c])[2]) for c in range(NC)]


def as_int(flag):
    return flag.astype(jnp.int32)


def kernel(flow, rates, out, q, s1, new, coef, halo, hk, rf, rb, rp,
           in_sem, out_sem, s_far, s_near, s_az, s_rel, r_halo, r_rel, r_az, far_sem, pole_sem, wrap_sem):
    mn, az = lax.axis_index("mn"), lax.axis_index("az")
    n_mn, n_az = lax.axis_size("mn"), lax.axis_size("az")
    groups = n_mn // COLUMNS
    x, m = lax.rem(mn, COLUMNS), lax.div(mn, COLUMNS)
    opp = lax.rem(az + n_az // 2, n_az)
    az_up, az_dn = lax.rem(az + 1, n_az), lax.rem(az + n_az - 1, n_az)
    pole = mn == 0
    first, last = x == 0, x == COLUMNS - 1
    up_far = last & (m < groups - 1)
    f_to = (4 * m + 4, az)
    b_to = (jnp.where(pole | (m == 0), 0, 4 * m - 1), jnp.where(m == 0, opp, az))
    b_side = jnp.where(m == 0, 0, 1)

    even, odd = lax.rem(m, 2) == 0, lax.rem(m, 2) == 1
    g0, g6 = m == 0, m == POLE_GROUP
    low_z, high_z = az < n_az // 2, az >= n_az // 2
    above = m < groups - 1
    not_first, not_last = jnp.logical_not(first), jnp.logical_not(last)
    back, back_or_pole = first & (m > 0), first
    wrap_dn, no_wrap_dn = az == 0, az > 0
    relays_f = [(x == p) & above for p in range(4)]
    relays_b = [(x == p) & (m > 0) for p in range(4)]
    relays_0 = [(x == p) & g0 for p in range(4)]
    relays_6 = [(x == p) & g6 for p in range(4)]
    bar = pltpu.get_barrier_semaphore()

    def tell(cond, device, sem=bar):
        def signal():
            pl.semaphore_signal(sem, 1, device_id=device, device_id_type=MESH)
        if cond is None:
            signal()
        else:
            pl.when(cond)(signal)

    for d in range(1, 4):
        tell(None, (4 * m + lax.rem(x + d, 4), az))
    tell(None, (mn, az_dn))
    tell(az < n_az - 1, (mn, az_up))
    tell(even, (4 * m + 4, az))
    tell(even & (m > 0), (4 * m - 1, az))
    for p in range(3):
        tell(even & first & (m > 0), (4 * m - 4 + p, az))
        tell(even & last, (4 * m + 5 + p, az))
        tell(pole & low_z, (p + 1, opp))
    tell((g0 | g6) & low_z, (0, opp))
    for p in range(4):
        tell(pole & low_z, (4 * POLE_GROUP + p, opp))
    tell(g6, (0, az))
    targets = 5 - as_int(az == 0) + 4 * as_int(pole) + as_int(odd) + 3 * as_int(odd & first)
    targets += as_int(odd & above) + 3 * as_int(odd & above & last)
    targets += 8 * as_int(pole & high_z) + as_int(((g0 & (x > 0)) | g6) & high_z)

    load = pltpu.make_async_copy(flow, q, in_sem)
    load.start()

    @pl.when(mn == n_mn - 1)
    def _():
        for e in range(2):
            halo[e, 1] = jnp.zeros((NQ, 2, ROWS, LANES), jnp.float32)


    def source(field, acc):
        def pair(t, _):
            a = 2 * t
            sums = [[None] * ROWS, [None] * ROWS]
            for b in range(NLEV):
                r0, r1 = rates[a, b], rates[a + 1, b]
                for i in range(ROWS):
                    v = field[FIRST_LEVEL + b, i]
                    for s, r in ((0, r0), (1, r1)):
                        term = v * r
                        sums[s][i] = term if b == 0 else sums[s][i] + term
            for i in range(ROWS):
                scale = TIME_STEP * field[ELECTRON, i]
                for s in range(2):
                    acc[FIRST_LEVEL + a + s, i] = scale * sums[s][i]
            return 0
        lax.fori_loop(0, NLEV // 2, pair, 0)

    pl.semaphore_wait(bar, targets)
    for p in range(4):
        tell(odd & first, (4 * m - 4 + p, az), far_sem)
        tell(odd & last & above, (4 * m + 4 + p, az), far_sem)
        tell(pole & high_z, (p, opp), pole_sem)
        tell(pole & high_z, (4 * POLE_GROUP + p, opp), pole_sem)
    tell(az == n_az - 1, (mn, az_up), wrap_sem)

    started = []

    def copy(src, dst, s, r, device):
        return pltpu.make_async_remote_copy(src, dst, s, r, device_id=device, device_id_type=MESH)

    def start(cond, *copies):
        def go():
            for c in copies:
                c.start()
        if cond is None:
            go()
        else:
            pl.when(cond)(go)
        started.append((cond, copies))

    def send_to_relays(e, c, field):
        _, _, ups, downs = CHUNKS[c]

        def handed(side, rows, to, p, group):
            a, b = (downs if side else ups)[p]
            return copy(field.at[a:b, rows:rows + 2], to.at[e, a:b], s_far.at[e, side, c, p], r_rel.at[e, side, c], (4 * group + p, az))

        start(up_far, *[handed(0, 6, rf, p, m) for p in range(3)])
        start(back if c in POLE_CHUNKS else back_or_pole, *[handed(1, 0, rb, p, m) for p in range(1, 4)])
        if c in POLE_CHUNKS:
            start(pole, *[handed(2, 0, rp, p, POLE_GROUP) for p in range(4)])

    def send_direct(e, c, field, across):
        _, _, ups, downs = CHUNKS[c]
        a, b = ups[3]
        if not across:
            start(up_far, copy(field.at[a:b, 6:8], halo.at[e, 0, a:b], s_far.at[e, 0, c, 3], r_halo.at[e, 0, c, 3], f_to))
        a, b = downs[0]
        if not across or c not in POLE_CHUNKS:
            cond = pole if across else back
            start(cond, copy(field.at[a:b, 0:2], halo.at[e, b_side, a:b], s_far.at[e, 1, c, 0], r_halo.at[e, b_side, c, 0], b_to))

    def az_copies(e, c, field):
        a, b, _, _ = CHUNKS[c]
        return (
            copy(field.at[a:b, :, 0:2], hk.at[e, a:b, :, 0:2], s_az.at[e, 0, c], r_az.at[e, 0, c], (mn, az_dn)),
            copy(field.at[a:b, :, 6:8], hk.at[e, a:b, :, 6:8], s_az.at[e, 1, c], r_az.at[e, 1, c], (mn, az_up)),
        )

    def send_az(e, c, field):
        start(None, *az_copies(e, c, field))

    def send_near(e, c, field):
        a, b, _, _ = CHUNKS[c]
        start(not_last, copy(field.at[a:b, 6:8], halo.at[e, 0, a:b], s_near.at[e, 0, c], r_halo.at[e, 0, c, 0], (mn + 1, az)))
        start(not_first, copy(field.at[a:b, 0:2], halo.at[e, 1, a:b], s_near.at[e, 1, c], r_halo.at[e, 1, c, 0], (mn - 1, az)))

    def await_copies(cond, *landed):
        def go():
            for dst, r in landed:
                copy(dst, dst, in_sem, r, f_to).wait_recv()
        if cond is None:
            go()
        else:
            pl.when(cond)(go)

    def relay(e, c, across):
        _, _, ups, downs = CHUNKS[c]

        def passed_on(cond, held, side, to, p, device):
            a, b = (downs if side else ups)[p]
            await_copies(cond, (held.at[e, a:b], r_rel.at[e, side, c]))
            start(cond, copy(held.at[e, a:b], halo.at[e, to, a:b], s_rel.at[e, side, c], r_halo.at[e, to, c, p], device))

        for p in range(4):
            if p != 3 and not across:
                passed_on(relays_f[p], rf, 0, 0, p, f_to)
            if p != 0 and not (across and c in POLE_CHUNKS):
                passed_on((relays_0 if across else relays_b)[p], rb, 1, b_side, p, b_to)
            if across and c in POLE_CHUNKS:
                passed_on(relays_6[p], rp, 2, 0, p, (0, opp))

    def await_margins(e, c):
        a, b, ups, downs = CHUNKS[c]
        await_copies(None, (hk.at[e, a:b, :, 0:2], r_az.at[e, 0, c]), (hk.at[e, a:b, :, 6:8], r_az.at[e, 1, c]))
        await_copies(not_first, (halo.at[e, 0, a:b], r_halo.at[e, 0, c, 0]))
        await_copies(not_last, (halo.at[e, 1, a:b], r_halo.at[e, 1, c, 0]))
        for cond, side, parts in ((back, 0, ups), (pole, 0, downs), (up_far, 1, downs)):
            await_copies(cond, *[(halo.at[e, side, pa:pb], r_halo.at[e, side, c, p]) for p, (pa, pb) in enumerate(parts)])
        if c == 0:
            @pl.when(pole)
            def _():
                for n in (5, 7):
                    halo[e, 0, n] = -halo[e, 0, n]

    below = (jnp.where(pole, 0, 1), jnp.where(pole, 1, 0))

    def row(e, field, n, i):
        if i < 0:
            return halo[e, 0, n, below[-i - 1]]
        if i >= ROWS:
            return halo[e, 1, n, i - ROWS]
        return field[n, i]

    k_at = lax.broadcasted_iota(jnp.int32, (ROWS, LANES), 0)
    j_at = lax.broadcasted_iota(jnp.int32, (ROWS, LANES), 1)

    def along_k(v, h):
        return [
            pltpu.roll(jnp.where(k_at < 1, h, v), 7, 0),
            pltpu.roll(jnp.where(k_at < 2, h, v), 6, 0),
            pltpu.roll(jnp.where(k_at >= 7, h, v), 1, 0),
            pltpu.roll(jnp.where(k_at >= 6, h, v), 2, 0),
        ]

    def speed(u, v):
        return DISSIPATION * (0.5 * (jnp.abs(u) + jnp.abs(v)) + SOUND_SPEED)

    def taps(u_m, u, u_p):
        s_m, s_p = speed(u_m, u), speed(u, u_p)
        return (
            TIME_STEP * (-0.5 * u_p - 3.0 * s_p - s_m),
            TIME_STEP * s_p,
            TIME_STEP * (0.5 * u_m - s_p - 3.0 * s_m),
            TIME_STEP * s_m,
            (3.0 * TIME_STEP) * (s_p + s_m),
        )

    def coefficients():
        def density(read):
            return 1.0 / jnp.maximum(read(0) + read(1) + read(2) + read(3) + read(4), 1.0)

        def u_i(i):
            return row(0, q, 5, i) * density(lambda n: row(0, q, n, i))

        u_m, u = u_i(-1), u_i(0)
        for i in range(ROWS):
            u_p = u_i(i + 1)
            inverse = density(lambda n: q[n, i])
            ti = taps(u_m, u, u_p)
            u_m, u = u, u_p
            uk = q[7, i] * inverse
            hk_u = hk[0, 7, i] * density(lambda n: hk[0, n, i])
            shifted = along_k(uk, hk_u)
            tk = taps(shifted[2], uk, shifted[0])
            uj = q[6, i] * inverse
            uj_p = jnp.where(j_at < LANES - 1, pltpu.roll(uj, LANES - 1, 1), 0.0)
            uj_m = jnp.where(j_at > 0, pltpu.roll(uj, 1, 1), 0.0)
            tj = taps(uj_m, uj, uj_p)
            for t in range(4):
                coef[t, i] = ti[t]
                coef[4 + t, i] = tk[t]
            coef[8, i] = jnp.where(j_at < LANES - 1, tj[0], 0.0)
            coef[9, i] = jnp.where(j_at < LANES - 2, tj[1], 0.0)
            coef[10, i] = jnp.where(j_at > 0, tj[2], 0.0)
            coef[11, i] = jnp.where(j_at > 1, tj[3], 0.0)
            coef[12, i] = 1.0 + ti[4] + tk[4] + tj[4]

    def section(e, field, acc, a, b, chemistry, final):
        for i in range(ROWS):
            cs = [coef[t, i] for t in range(13)]

            def one(n):
                v = field[n, i]
                ks = along_k(v, hk[e, n, i])
                js = [pltpu.roll(v, (LANES - d) % LANES, 1) for d in (1, 2, -1, -2)]
                rows = [row(e, field, n, i + d) for d in (1, 2, -1, -2)]
                sums = [cs[12] * v]
                for base, values in ((0, rows), (4, ks), (8, js)):
                    t = [cs[base + d] * values[d] for d in range(4)]
                    sums.append((t[0] + t[1]) + (t[2] + t[3]))
                r = (sums[0] + sums[1]) + (sums[2] + sums[3])
                if chemistry:
                    r = r + acc[n, i]
                acc[n, i] = 0.5 * r if final else r

            for n in range(a, b):
                one(n)

    load.wait()
    for c in range(NC):
        send_to_relays(0, c, q)
    for c in range(NC):
        down, up = az_copies(0, c, q)
        start(no_wrap_dn, down)
        start(None, up)
    for c in range(NC):
        send_near(0, c, q)
    source(q, s1)

    @pl.when((g0 | g6) & low_z)
    def _():
        pl.semaphore_wait(pole_sem, 1)

    for c in range(NC):
        send_direct(0, c, q, True)
    for c in range(NC):
        relay(0, c, True)

    @pl.when(az == 0)
    def _():
        pl.semaphore_wait(wrap_sem, 1)

    for c in range(NC):
        start(wrap_dn, az_copies(0, c, q)[0])

    @pl.when(even)
    def _():
        pl.semaphore_wait(far_sem, 1 + as_int(m > 0))

    for c in range(NC):
        send_direct(0, c, q, False)
    for c in range(NC):
        relay(0, c, False)
    for c in range(NC):
        a, b, _, _ = CHUNKS[c]
        await_margins(0, c)
        if c == 0:
            coefficients()
        section(0, q, s1, a, b, c > 0, False)
        send_to_relays(1, c, s1)
        send_direct(1, c, s1, True)
        send_direct(1, c, s1, False)
        send_az(1, c, s1)
        send_near(1, c, s1)
        if c >= LAG:
            relay(1, c - LAG, True)
            relay(1, c - LAG, False)
    for c in range(NC - LAG, NC):
        relay(1, c, True)
        relay(1, c, False)
    source(s1, new)
    stores = []
    for c in range(NC):
        a, b, _, _ = CHUNKS[c]
        await_margins(1, c)
        section(1, s1, new, a, b, c > 0, True)
        store = pltpu.make_async_copy(new.at[a:b], out.at[a:b], out_sem.at[c])
        store.start()
        stores.append(store)
    groups_of = {}
    for cond, copies in started:
        groups_of.setdefault(id(cond), (cond, []))[1].extend(copies)
    for cond, copies in groups_of.values():
        def go(copies=copies):
            for c in copies:
                c.wait_send()
        if cond is None:
            go()
        else:
            pl.when(cond)(go)
    for store in stores:
        store.wait()


def on_device(flow_state, level_rates):
    def vmem(*shape):
        return pltpu.VMEM(shape, jnp.float32)

    def sems(*shape):
        return pltpu.SemaphoreType.DMA(shape)

    block = (NQ, ROWS, ROWS, LANES)
    margin = (NQ, 2, ROWS, LANES)
    half = pl.pallas_call(
        kernel,
        out_shape=jax.ShapeDtypeStruct(block, jnp.float32),
        in_specs=[pl.BlockSpec(memory_space=pl.ANY), pl.BlockSpec(memory_space=pltpu.SMEM)],
        out_specs=pl.BlockSpec(memory_space=pl.ANY),
        scratch_shapes=[
            vmem(*block), vmem(*block), vmem(*block), vmem(13, ROWS, ROWS, LANES),
            vmem(2, 2, *margin), vmem(2, *block), vmem(2, *margin), vmem(2, *margin), vmem(2, *margin),
            pltpu.SemaphoreType.DMA, sems(NC), sems(2, 3, NC, 4), sems(2, 2, NC), sems(2, 2, NC), sems(2, 3, NC),
            sems(2, 2, NC, 4), sems(2, 3, NC), sems(2, 2, NC),
            pltpu.SemaphoreType.REGULAR, pltpu.SemaphoreType.REGULAR, pltpu.SemaphoreType.REGULAR,
        ],
        compiler_params=pltpu.CompilerParams(
            collective_id=0, has_side_effects=True, vmem_limit_bytes=VMEM_LIMIT
        ),
    )(flow_state, level_rates)
    return 0.5 * flow_state + half


def solution(mesh):
    in_specs = (P(None, "mn", "az", None), P())
    out_specs = P(None, "mn", "az", None)
    return jax.shard_map(
        on_device, mesh=mesh, in_specs=in_specs, out_specs=out_specs, check_vma=False
    )
```

```python
import functools

import jax
import jax.numpy as jnp
from jax import lax
from jax.experimental import pallas as pl
from jax.experimental.pallas import tpu as pltpu
from jax.sharding import PartitionSpec as P

MESH = pl.DeviceIdType.MESH
DISSIPATION = 0.05
SOUND_SPEED = 1.0
TIME_STEP = 0.3
NQ, NLEV, FIRST_LEVEL, ELECTRON = 41, 30, 11, 10
ROWS, LANES = 8, 128
COLUMNS = 4
VMEM_LIMIT = 60 * 1024 * 1024
UP_SIZES = ((3, 3, 3, 2), (4, 3, 4, 4), (3, 4, 4, 4))
DOWN_SIZES = ((3, 3, 3, 2), (3, 4, 4, 4), (4, 4, 3, 4))
LAG = 1
INNER, OUTER = (2, 3, 4, 5), (0, 1, 6, 7)
POLE_GROUP, POLE_CHUNKS = 6, (0, 2)


def cuts(start, sizes):
    bounds = [start + sum(sizes[:p]) for p in range(COLUMNS + 1)]
    return bounds[0], bounds[-1], list(zip(bounds[:-1], bounds[1:]))


NC = len(UP_SIZES)
STARTS = [sum(sum(sizes) for sizes in UP_SIZES[:c]) for c in range(NC)]
CHUNKS = [(*cuts(STARTS[c], UP_SIZES[c]), cuts(STARTS[c], DOWN_SIZES[c])[2]) for c in range(NC)]


def as_int(flag):
    return flag.astype(jnp.int32)


def kernel(flow, rates, out, q, s1, new, coef, halo, hk, rf, rb, rp,
           in_sem, out_sem, s_far, s_near, s_az, s_rel, r_halo, r_rel, r_az, far_sem, pole_sem, wrap_sem):
    mn, az = lax.axis_index("mn"), lax.axis_index("az")
    n_mn, n_az = lax.axis_size("mn"), lax.axis_size("az")
    groups = n_mn // COLUMNS
    x, m = lax.rem(mn, COLUMNS), lax.div(mn, COLUMNS)
    opp = lax.rem(az + n_az // 2, n_az)
    az_up, az_dn = lax.rem(az + 1, n_az), lax.rem(az + n_az - 1, n_az)
    pole = mn == 0
    first, last = x == 0, x == COLUMNS - 1
    up_far = last & (m < groups - 1)
    f_to = (4 * m + 4, az)
    b_to = (jnp.where(pole | (m == 0), 0, 4 * m - 1), jnp.where(m == 0, opp, az))
    b_side = jnp.where(m == 0, 0, 1)

    even, odd = lax.rem(m, 2) == 0, lax.rem(m, 2) == 1
    g0, g6 = m == 0, m == POLE_GROUP
    low_z, high_z = az < n_az // 2, az >= n_az // 2
    above = m < groups - 1
    not_first, not_last = jnp.logical_not(first), jnp.logical_not(last)
    back, back_or_pole = first & (m > 0), first
    wrap_dn, no_wrap_dn = az == 0, az > 0
    relays_f = [(x == p) & above for p in range(4)]
    relays_b = [(x == p) & (m > 0) for p in range(4)]
    relays_0 = [(x == p) & g0 for p in range(4)]
    relays_6 = [(x == p) & g6 for p in range(4)]
    bar = pltpu.get_barrier_semaphore()

    def tell(cond, device, sem=bar):
        def signal():
            pl.semaphore_signal(sem, 1, device_id=device, device_id_type=MESH)
        if cond is None:
            signal()
        else:
            pl.when(cond)(signal)

    for d in range(1, 4):
        tell(None, (4 * m + lax.rem(x + d, 4), az))
    tell(None, (mn, az_dn))
    tell(az < n_az - 1, (mn, az_up))
    tell(even, (4 * m + 4, az))
    tell(even & (m > 0), (4 * m - 1, az))
    for p in range(3):
        tell(even & first & (m > 0), (4 * m - 4 + p, az))
        tell(even & last, (4 * m + 5 + p, az))
        tell(pole & low_z, (p + 1, opp))
    tell((g0 | g6) & low_z, (0, opp))
    for p in range(4):
        tell(pole & low_z, (4 * POLE_GROUP + p, opp))
    tell(g6, (0, az))
    targets = 5 - as_int(az == 0) + 4 * as_int(pole) + as_int(odd) + 3 * as_int(odd & first)
    targets += as_int(odd & above) + 3 * as_int(odd & above & last)
    targets += 8 * as_int(pole & high_z) + as_int(((g0 & (x > 0)) | g6) & high_z)

    load = pltpu.make_async_copy(flow, q, in_sem)
    load.start()

    @pl.when(mn == n_mn - 1)
    def _():
        for e in range(2):
            halo[e, 1] = jnp.zeros((NQ, 2, ROWS, LANES), jnp.float32)


    def source(field, acc):
        def pair(t, _):
            a = 2 * t
            sums = [[None] * ROWS, [None] * ROWS]
            for b in range(NLEV):
                r0, r1 = rates[a, b], rates[a + 1, b]
                for i in range(ROWS):
                    v = field[FIRST_LEVEL + b, i]
                    for s, r in ((0, r0), (1, r1)):
                        term = v * r
                        sums[s][i] = term if b == 0 else sums[s][i] + term
            for i in range(ROWS):
                scale = TIME_STEP * field[ELECTRON, i]
                for s in range(2):
                    acc[FIRST_LEVEL + a + s, i] = scale * sums[s][i]
            return 0
        lax.fori_loop(0, NLEV // 2, pair, 0)

    pl.semaphore_wait(bar, targets)
    for p in range(4):
        tell(odd & first, (4 * m - 4 + p, az), far_sem)
        tell(odd & last & above, (4 * m + 4 + p, az), far_sem)
        tell(pole & high_z, (p, opp), pole_sem)
        tell(pole & high_z, (4 * POLE_GROUP + p, opp), pole_sem)
    tell(az == n_az - 1, (mn, az_up), wrap_sem)

    started = []

    def copy(src, dst, s, r, device):
        return pltpu.make_async_remote_copy(src, dst, s, r, device_id=device, device_id_type=MESH)

    def start(cond, *copies):
        def go():
            for c in copies:
                c.start()
        if cond is None:
            go()
        else:
            pl.when(cond)(go)
        started.append((cond, copies))

    def send_to_relays(e, c, field):
        _, _, ups, downs = CHUNKS[c]

        def handed(side, rows, to, p, group):
            a, b = (downs if side else ups)[p]
            return copy(field.at[a:b, rows:rows + 2], to.at[e, a:b], s_far.at[e, side, c, p], r_rel.at[e, side, c], (4 * group + p, az))

        start(up_far, *[handed(0, 6, rf, p, m) for p in range(3)])
        start(back if c in POLE_CHUNKS else back_or_pole, *[handed(1, 0, rb, p, m) for p in range(1, 4)])
        if c in POLE_CHUNKS:
            start(pole, *[handed(2, 0, rp, p, POLE_GROUP) for p in range(4)])

    def send_direct(e, c, field, across):
        _, _, ups, downs = CHUNKS[c]
        a, b = ups[3]
        if not across:
            start(up_far, copy(field.at[a:b, 6:8], halo.at[e, 0, a:b], s_far.at[e, 0, c, 3], r_halo.at[e, 0, c, 3], f_to))
        a, b = downs[0]
        if not across or c not in POLE_CHUNKS:
            cond = pole if across else back
            start(cond, copy(field.at[a:b, 0:2], halo.at[e, b_side, a:b], s_far.at[e, 1, c, 0], r_halo.at[e, b_side, c, 0], b_to))

    def az_copies(e, c, field):
        a, b, _, _ = CHUNKS[c]
        return (
            copy(field.at[a:b, :, 0:2], hk.at[e, a:b, :, 0:2], s_az.at[e, 0, c], r_az.at[e, 0, c], (mn, az_dn)),
            copy(field.at[a:b, :, 6:8], hk.at[e, a:b, :, 6:8], s_az.at[e, 1, c], r_az.at[e, 1, c], (mn, az_up)),
        )

    def send_az(e, c, field):
        start(None, *az_copies(e, c, field))

    def send_near(e, c, field):
        a, b, _, _ = CHUNKS[c]
        start(not_last, copy(field.at[a:b, 6:8], halo.at[e, 0, a:b], s_near.at[e, 0, c], r_halo.at[e, 0, c, 0], (mn + 1, az)))
        start(not_first, copy(field.at[a:b, 0:2], halo.at[e, 1, a:b], s_near.at[e, 1, c], r_halo.at[e, 1, c, 0], (mn - 1, az)))

    def await_copies(cond, *landed):
        def go():
            for dst, r in landed:
                copy(dst, dst, in_sem, r, f_to).wait_recv()
        if cond is None:
            go()
        else:
            pl.when(cond)(go)

    def relay(e, c, across):
        _, _, ups, downs = CHUNKS[c]

        def passed_on(cond, held, side, to, p, device):
            a, b = (downs if side else ups)[p]
            await_copies(cond, (held.at[e, a:b], r_rel.at[e, side, c]))
            start(cond, copy(held.at[e, a:b], halo.at[e, to, a:b], s_rel.at[e, side, c], r_halo.at[e, to, c, p], device))

        for p in range(4):
            if p != 3 and not across:
                passed_on(relays_f[p], rf, 0, 0, p, f_to)
            if p != 0 and not (across and c in POLE_CHUNKS):
                passed_on((relays_0 if across else relays_b)[p], rb, 1, b_side, p, b_to)
            if across and c in POLE_CHUNKS:
                passed_on(relays_6[p], rp, 2, 0, p, (0, opp))

    def await_near(e, c):
        a, b, _, _ = CHUNKS[c]
        await_copies(None, (hk.at[e, a:b, :, 0:2], r_az.at[e, 0, c]), (hk.at[e, a:b, :, 6:8], r_az.at[e, 1, c]))
        await_copies(not_first, (halo.at[e, 0, a:b], r_halo.at[e, 0, c, 0]))
        await_copies(not_last, (halo.at[e, 1, a:b], r_halo.at[e, 1, c, 0]))

    def await_far(e, c):
        _, _, ups, downs = CHUNKS[c]
        for cond, side, parts in ((back, 0, ups), (pole, 0, downs), (up_far, 1, downs)):
            await_copies(cond, *[(halo.at[e, side, pa:pb], r_halo.at[e, side, c, p]) for p, (pa, pb) in enumerate(parts)])
        if c == 0:
            @pl.when(pole)
            def _():
                for n in (5, 7):
                    halo[e, 0, n] = -halo[e, 0, n]

    below = (jnp.where(pole, 0, 1), jnp.where(pole, 1, 0))

    def row(e, field, n, i):
        if i < 0:
            return halo[e, 0, n, below[-i - 1]]
        if i >= ROWS:
            return halo[e, 1, n, i - ROWS]
        return field[n, i]

    k_at = lax.broadcasted_iota(jnp.int32, (ROWS, LANES), 0)
    j_at = lax.broadcasted_iota(jnp.int32, (ROWS, LANES), 1)

    def along_k(v, h):
        return [
            pltpu.roll(jnp.where(k_at < 1, h, v), 7, 0),
            pltpu.roll(jnp.where(k_at < 2, h, v), 6, 0),
            pltpu.roll(jnp.where(k_at >= 7, h, v), 1, 0),
            pltpu.roll(jnp.where(k_at >= 6, h, v), 2, 0),
        ]

    def speed(u, v):
        return DISSIPATION * (0.5 * (jnp.abs(u) + jnp.abs(v)) + SOUND_SPEED)

    def taps(u_m, u, u_p):
        s_m, s_p = speed(u_m, u), speed(u, u_p)
        return (
            TIME_STEP * (-0.5 * u_p - 3.0 * s_p - s_m),
            TIME_STEP * s_p,
            TIME_STEP * (0.5 * u_m - s_p - 3.0 * s_m),
            TIME_STEP * s_m,
            (3.0 * TIME_STEP) * (s_p + s_m),
        )

    def coefficients(rows):
        def density(read):
            return 1.0 / jnp.maximum(read(0) + read(1) + read(2) + read(3) + read(4), 1.0)

        def u_i(i):
            return row(0, q, 5, i) * density(lambda n: row(0, q, n, i))

        for i in rows:
            inverse = density(lambda n: q[n, i])
            ti = taps(u_i(i - 1), q[5, i] * inverse, u_i(i + 1))
            uk = q[7, i] * inverse
            hk_u = hk[0, 7, i] * density(lambda n: hk[0, n, i])
            shifted = along_k(uk, hk_u)
            tk = taps(shifted[2], uk, shifted[0])
            uj = q[6, i] * inverse
            uj_p = jnp.where(j_at < LANES - 1, pltpu.roll(uj, LANES - 1, 1), 0.0)
            uj_m = jnp.where(j_at > 0, pltpu.roll(uj, 1, 1), 0.0)
            tj = taps(uj_m, uj, uj_p)
            for t in range(4):
                coef[t, i] = ti[t]
                coef[4 + t, i] = tk[t]
            coef[8, i] = jnp.where(j_at < LANES - 1, tj[0], 0.0)
            coef[9, i] = jnp.where(j_at < LANES - 2, tj[1], 0.0)
            coef[10, i] = jnp.where(j_at > 0, tj[2], 0.0)
            coef[11, i] = jnp.where(j_at > 1, tj[3], 0.0)
            coef[12, i] = 1.0 + ti[4] + tk[4] + tj[4]

    def section(e, field, acc, rows, a, b, chemistry, final):
        for i in rows:
            cs = [coef[t, i] for t in range(13)]

            def one(n):
                v = field[n, i]
                ks = along_k(v, hk[e, n, i])
                js = [pltpu.roll(v, (LANES - d) % LANES, 1) for d in (1, 2, -1, -2)]
                along_i = [row(e, field, n, i + d) for d in (1, 2, -1, -2)]
                sums = [cs[12] * v]
                for base, values in ((0, along_i), (4, ks), (8, js)):
                    t = [cs[base + d] * values[d] for d in range(4)]
                    sums.append((t[0] + t[1]) + (t[2] + t[3]))
                r = (sums[0] + sums[1]) + (sums[2] + sums[3])
                if chemistry:
                    r = r + acc[n, i]
                acc[n, i] = 0.5 * r if final else r

            for n in range(a, b):
                one(n)

    load.wait()
    for c in range(NC):
        send_to_relays(0, c, q)
    for c in range(NC):
        down, up = az_copies(0, c, q)
        start(no_wrap_dn, down)
        start(None, up)
    for c in range(NC):
        send_near(0, c, q)
    source(q, s1)

    @pl.when((g0 | g6) & low_z)
    def _():
        pl.semaphore_wait(pole_sem, 1)

    for c in range(NC):
        send_direct(0, c, q, True)
    for c in range(NC):
        relay(0, c, True)

    @pl.when(az == 0)
    def _():
        pl.semaphore_wait(wrap_sem, 1)

    for c in range(NC):
        start(wrap_dn, az_copies(0, c, q)[0])

    @pl.when(even)
    def _():
        pl.semaphore_wait(far_sem, 1 + as_int(m > 0))

    for c in range(NC):
        send_direct(0, c, q, False)
    for c in range(NC):
        relay(0, c, False)
    for c in range(NC):
        a, b, _, _ = CHUNKS[c]
        await_near(0, c)
        if c == 0:
            coefficients(INNER)
        section(0, q, s1, INNER, a, b, c > 0, False)
        await_far(0, c)
        if c == 0:
            coefficients(OUTER)
        section(0, q, s1, OUTER, a, b, c > 0, False)
        send_to_relays(1, c, s1)
        send_direct(1, c, s1, True)
        send_direct(1, c, s1, False)
        send_az(1, c, s1)
        send_near(1, c, s1)
        if c >= LAG:
            relay(1, c - LAG, True)
            relay(1, c - LAG, False)
    for c in range(NC - LAG, NC):
        relay(1, c, True)
        relay(1, c, False)
    source(s1, new)
    stores = []
    for c in range(NC):
        a, b, _, _ = CHUNKS[c]
        await_near(1, c)
        section(1, s1, new, INNER, a, b, c > 0, True)
        await_far(1, c)
        section(1, s1, new, OUTER, a, b, c > 0, True)
        store = pltpu.make_async_copy(new.at[a:b], out.at[a:b], out_sem.at[c])
        store.start()
        stores.append(store)
    groups_of = {}
    for cond, copies in started:
        groups_of.setdefault(id(cond), (cond, []))[1].extend(copies)
    for cond, copies in groups_of.values():
        def go(copies=copies):
            for c in copies:
                c.wait_send()
        if cond is None:
            go()
        else:
            pl.when(cond)(go)
    for store in stores:
        store.wait()


def on_device(flow_state, level_rates):
    def vmem(*shape):
        return pltpu.VMEM(shape, jnp.float32)

    def sems(*shape):
        return pltpu.SemaphoreType.DMA(shape)

    block = (NQ, ROWS, ROWS, LANES)
    margin = (NQ, 2, ROWS, LANES)
    half = pl.pallas_call(
        kernel,
        out_shape=jax.ShapeDtypeStruct(block, jnp.float32),
        in_specs=[pl.BlockSpec(memory_space=pl.ANY), pl.BlockSpec(memory_space=pltpu.SMEM)],
        out_specs=pl.BlockSpec(memory_space=pl.ANY),
        scratch_shapes=[
            vmem(*block), vmem(*block), vmem(*block), vmem(13, ROWS, ROWS, LANES),
            vmem(2, 2, *margin), vmem(2, *block), vmem(2, *margin), vmem(2, *margin), vmem(2, *margin),
            pltpu.SemaphoreType.DMA, sems(NC), sems(2, 3, NC, 4), sems(2, 2, NC), sems(2, 2, NC), sems(2, 3, NC),
            sems(2, 2, NC, 4), sems(2, 3, NC), sems(2, 2, NC),
            pltpu.SemaphoreType.REGULAR, pltpu.SemaphoreType.REGULAR, pltpu.SemaphoreType.REGULAR,
        ],
        compiler_params=pltpu.CompilerParams(
            collective_id=0, has_side_effects=True, vmem_limit_bytes=VMEM_LIMIT
        ),
    )(flow_state, level_rates)
    return 0.5 * flow_state + half


def solution(mesh):
    in_specs = (P(None, "mn", "az", None), P())
    out_specs = P(None, "mn", "az", None)
    return jax.shard_map(
        on_device, mesh=mesh, in_specs=in_specs, out_specs=out_specs, check_vma=False
    )
```
